256 devices in a mesh: rep: 2 (over x_hi), ew: 8 (over z), ns: 16 (over x_lo, y, core).
Axes of the slice: x: 4 (x_hi: 2, x_lo: 2; x = x_hi * 2 + x_lo), y: 4, z: 8, core: 2. Of those that a mesh axis runs over, the one named last changes fastest.
Arguments:
- fields: bfloat16 [2, 192, 32, 2048], P('rep', None, 'ew', 'ns'), may hold values from -6 to 6
- cotangent: bfloat16 [2, 192, 32, 2048], P('rep', None, 'ew', 'ns'), may hold values from -6 to 6
- land_mask: int32 [32, 2048], P('ew', 'ns'), may hold values 0 or 1
- stretch_index: int32 [1], replicated, may hold values from 0 to 23
- depth_kernel: float32 [2, 2, 192, 49], P('rep'), may hold values from -0.875 to 0.875
- norm_gain: float32 [2, 2, 192], P('rep'), may hold values from 0.5 to 1.5
- norm_bias: float32 [2, 2, 192], P('rep'), may hold values from -3 to 3
- weight_in: float32 [2, 2, 192, 768], P('rep'), may hold values from -0.4375 to 0.4375
- bias_in: float32 [2, 2, 768], P('rep'), may hold values from -3 to 3
- weight_out: float32 [2, 2, 768, 192], P('rep'), may hold values from -0.21875 to 0.21875
- bias_out: float32 [2, 2, 192], P('rep'), may hold values from -3 to 3
- layer_scale: float32 [2, 2, 192], P('rep'), may hold values from 0.5 to 1.5
- anchor_in: float32 [2, 192, 768], replicated, may hold values from -0.4375 to 0.4375
- anchor_out: float32 [2, 768, 192], replicated, may hold values from -0.21875 to 0.21875
Outputs:
- new_kernel: float32 [2, 2, 192, 49], P('rep')
- new_weight_in: float32 [2, 2, 192, 768], P('rep')
- new_weight_out: float32 [2, 2, 768, 192], P('rep')
- cycle_in: float32 [2, 192, 64], P('rep')
- cycle_out: float32 [2, 64, 192], P('rep')
The draws below stay inside these ranges and needn't reach their ends.
All inputs are finite; a program needn't handle non-finite values. No bound on the sum of `land_mask` on one device may be relied on, other than what follows from the above.
Results may differ from the reference program's by a relative error of at most 0.007.
Values may be sent and summed in bfloat16 or wider, within the bound.
A program may use at most 128 MiB of HBM per device.

```python
import math
import jax
import jax.numpy as jnp
from jax import lax

C = 192
HID = 768
LAYERS = 2
STRETCHES = 12
SPAN = 64
CX = 4
REPS = 2
NX = 32
NY = 2048


def plant(values, rng, low, high):
    spot = [jax.random.randint(jax.random.fold_in(rng, axis), (), 0, length) for axis, length in enumerate(values.shape)]
    main_axis = values.shape.index(max(values.shape))
    next_to = spot[:main_axis] + [(spot[main_axis] + 1) % values.shape[main_axis]] + spot[main_axis + 1:]
    return values.at[tuple(spot)].set(low).at[tuple(next_to)].set(high)


def steps_of(stream_key, extent, cuts, least, high):
    def one(position, shards_of):
        steps = jax.random.uniform(jax.random.fold_in(jax.random.fold_in(stream_key, 6), position), (shards_of,), jnp.float32, least / len(cuts), high / len(cuts))
        return jnp.repeat(jnp.exp(steps), extent[position] // shards_of).reshape((-1,) + (1,) * (len(extent) - position - 1))

    loudness = one(*cuts[0])
    for cut in cuts[1:]:
        loudness = loudness * one(*cut)
    return loudness


def bell_draw(stream_key, shape, spread, reach, cuts=(), kind=jnp.bfloat16):
    array = spread * jax.random.normal(stream_key, shape, jnp.float32)
    if cuts:
        array = array * steps_of(stream_key, shape, cuts, -0.22, 0.18)
    return jnp.clip(array, -reach, reach).astype(kind)


def setup_inputs(seed: int = 0) -> dict:
    streams_of = jax.random.split(jax.random.key(seed), 15)
    fields = bell_draw(streams_of[0], (REPS, C, NX, NY), 1.0, 6.0, ((0, 2), (2, 8), (3, 16)))
    cotangent = bell_draw(streams_of[1], (REPS, C, NX, NY), 1.0, 6.0, ((0, 2), (2, 8), (3, 16)))
    land_mask = plant((jax.random.randint(streams_of[2], (NX, NY), 0, 10) < 7).astype(jnp.int32), jax.random.fold_in(streams_of[2], 1), 0, 1)
    stretch_index = jax.random.randint(streams_of[3], (1,), 0, LAYERS * STRETCHES).astype(jnp.int32)
    depth_kernel = bell_draw(streams_of[4], (REPS, LAYERS, C, 49), 49 ** -0.5, 0.875, ((0, 2),), jnp.float32)
    norm_gain = jnp.clip(1.0 + 0.1 * jax.random.normal(streams_of[5], (REPS, LAYERS, C), jnp.float32), 0.5, 1.5)
    norm_bias = bell_draw(streams_of[6], (REPS, LAYERS, C), 0.5, 3.0, ((0, 2),), jnp.float32)
    weight_in = bell_draw(streams_of[7], (REPS, LAYERS, C, HID), C ** -0.5, 0.4375, ((0, 2),), jnp.float32)
    bias_in = bell_draw(streams_of[8], (REPS, LAYERS, HID), 0.5, 3.0, ((0, 2),), jnp.float32)
    weight_out = bell_draw(streams_of[9], (REPS, LAYERS, HID, C), HID ** -0.5, 0.21875, ((0, 2),), jnp.float32)
    bias_out = bell_draw(streams_of[10], (REPS, LAYERS, C), 0.5, 3.0, ((0, 2),), jnp.float32)
    layer_scale = jnp.clip(0.5 + 1.0 * jax.random.uniform(streams_of[11], (REPS, LAYERS, C), jnp.float32) ** steps_of(streams_of[11], (REPS, LAYERS, C), ((0, 2),), -0.2, 0.2), 0.5, 1.5)
    anchor_in = bell_draw(streams_of[12], (LAYERS, C, HID), C ** -0.5, 0.4375, (), jnp.float32)
    anchor_out = bell_draw(streams_of[13], (LAYERS, HID, C), HID ** -0.5, 0.21875, (), jnp.float32)
    return {"fields": fields, "cotangent": cotangent, "land_mask": land_mask, "stretch_index": stretch_index, "depth_kernel": depth_kernel, "norm_gain": norm_gain, "norm_bias": norm_bias, "weight_in": weight_in, "bias_in": bias_in, "weight_out": weight_out, "bias_out": bias_out, "layer_scale": layer_scale, "anchor_in": anchor_in, "anchor_out": anchor_out}


EPSILON = 1e-06
STEP_RATE = 0.1
GELU_C = 0.7978845608028654

def depthwise(padded, kernel, extent_x, extent_y):
    summed = jnp.zeros((padded.shape[0], extent_x, extent_y), jnp.float32)
    for tap_row in range(7):
        for tap_col in range(7):
            weight_tap = kernel[:, tap_row * 7 + tap_col][:, None, None]
            summed = summed + weight_tap * padded[:, tap_row:tap_row + extent_x, tap_col:tap_col + extent_y]
    return summed

def kernel_grad(padded, conv_grad):
    extent_x = conv_grad.shape[1]
    extent_y = conv_grad.shape[2]
    columns = []
    for tap_row in range(7):
        for tap_col in range(7):
            window = padded[:, tap_row:tap_row + extent_x, tap_col:tap_col + extent_y]
            columns.append(lax.optimization_barrier(jnp.sum(conv_grad * window, axis=(1, 2))))
    return jnp.stack(columns, axis=1)

def gelu_pair(hidden_pre):
    tanh_arg = GELU_C * (hidden_pre + 0.044715 * hidden_pre * hidden_pre * hidden_pre)
    tanh_val = jnp.tanh(tanh_arg)
    gelu_value = 0.5 * hidden_pre * (1.0 + tanh_val)
    gelu_slope = 0.5 * (1.0 + tanh_val) + 0.5 * hidden_pre * (1.0 - tanh_val * tanh_val) * GELU_C * (1.0 + 3.0 * 0.044715 * hidden_pre * hidden_pre)
    return (gelu_value, gelu_slope)

def pointwise_forward(conv_out, residual, ocean_cells, gain_vec, shift_bias, weight_in_b, bias_vec_in, weight_out_b, bias_vec_out, scale_vec):
    centered = conv_out - lax.optimization_barrier(jnp.mean(conv_out, axis=0, keepdims=True))
    inv_std = lax.rsqrt(lax.optimization_barrier(jnp.mean(centered * centered, axis=0, keepdims=True)) + EPSILON)
    normed = centered * inv_std
    normed_b = (normed * gain_vec[:, None] + shift_bias[:, None]).astype(jnp.bfloat16)
    hidden_pre = jnp.dot(weight_in_b.T, normed_b, preferred_element_type=jnp.float32) + bias_vec_in[:, None]
    active, gelu_slope = gelu_pair(hidden_pre)
    active_b = active.astype(jnp.bfloat16)
    branch = jnp.dot(weight_out_b.T, active_b, preferred_element_type=jnp.float32) + bias_vec_out[:, None]
    output = ocean_cells[None, :] * (residual + scale_vec[:, None] * branch)
    return (output, (normed, inv_std, normed_b, gelu_slope, active_b))

def pointwise_backward(flow_grad, kept_values, ocean_cells, gain_vec, weight_in_b, weight_out_b, scale_vec):
    normed, inv_std, normed_b, gelu_slope, active_b = kept_values
    masked = ocean_cells[None, :] * flow_grad
    branch_grad = (masked * scale_vec[:, None]).astype(jnp.bfloat16)
    grad_out_w = jnp.dot(active_b, branch_grad.T, preferred_element_type=jnp.float32)
    active_grad = jnp.dot(weight_out_b, branch_grad, preferred_element_type=jnp.float32)
    hidden_grad = (active_grad * gelu_slope).astype(jnp.bfloat16)
    grad_in_w = jnp.dot(normed_b, hidden_grad.T, preferred_element_type=jnp.float32)
    normed_grad = jnp.dot(weight_in_b, hidden_grad, preferred_element_type=jnp.float32) * gain_vec[:, None]
    mean_grad = lax.optimization_barrier(jnp.mean(normed_grad, axis=0, keepdims=True))
    mean_cross = lax.optimization_barrier(jnp.mean(normed_grad * normed, axis=0, keepdims=True))
    conv_grad = inv_std * (normed_grad - mean_grad - normed * mean_cross)
    return (conv_grad, masked, grad_in_w, grad_out_w)

def pad_field(field):
    zeroed = jnp.pad(field, ((0, 0), (0, 0), (3, 3)))
    return jnp.pad(zeroed, ((0, 0), (3, 3), (0, 0)), mode='wrap')

def pick_stretch(anchor_inner, anchor_outer, inner_stack, outer_stack, choose):
    layer_pick = (choose // STRETCHES).astype(jnp.int32)
    start = (choose % STRETCHES * SPAN).astype(jnp.int32)
    diff_inner = lax.dynamic_index_in_dim(anchor_inner, layer_pick, 0, False) - lax.dynamic_index_in_dim(inner_stack, layer_pick, 0, False)
    diff_outer = lax.dynamic_index_in_dim(anchor_outer, layer_pick, 0, False) - lax.dynamic_index_in_dim(outer_stack, layer_pick, 0, False)
    return (lax.dynamic_slice_in_dim(diff_inner, start, SPAN, 1), lax.dynamic_slice_in_dim(diff_outer, start, SPAN, 0))

def reference(fields, cotangent, land_mask, stretch_index, depth_kernel, norm_gain, norm_bias, weight_in, bias_in, weight_out, bias_out, layer_scale, anchor_in, anchor_out):
    channels = fields.shape[1]
    blocks = NX // CX
    rescale = 1.0 / math.sqrt(NX * NY)
    ocean_cells = land_mask.astype(jnp.float32)
    ocean_blocks = ocean_cells.reshape(blocks, CX * NY)

    def to_blocks(source):
        return source.reshape(channels, blocks, CX, NY).transpose(1, 0, 2, 3).reshape(blocks, channels, CX * NY)

    def from_blocks(source):
        return source.reshape(blocks, channels, CX, NY).transpose(1, 0, 2, 3).reshape(channels, NX, NY)
    kernels_all, inner_all, outer_all, stretch_inner, stretch_outer = ([], [], [], [], [])
    choose = stretch_index[0]
    for replica in range(REPS):
        current = fields[replica]
        stored = []
        for layer_index in range(LAYERS):
            kernel = depth_kernel[replica, layer_index]
            gain_vec = norm_gain[replica, layer_index]
            shift_bias = norm_bias[replica, layer_index]
            weight_in_b = weight_in[replica, layer_index].astype(jnp.bfloat16)
            bias_vec_in = bias_in[replica, layer_index]
            weight_out_b = weight_out[replica, layer_index].astype(jnp.bfloat16)
            bias_vec_out = bias_out[replica, layer_index]
            scale_vec = layer_scale[replica, layer_index]
            layer_in = current.astype(jnp.float32)
            padded = pad_field(layer_in)
            conv_out = depthwise(padded, kernel, NX, NY)

            def forward_block(block_items):
                conv_block, resid_block, ocean_block = block_items
                output, kept_values = pointwise_forward(conv_block, resid_block, ocean_block, gain_vec, shift_bias, weight_in_b, bias_vec_in, weight_out_b, bias_vec_out, scale_vec)
                return output
            output = from_blocks(lax.map(forward_block, (to_blocks(conv_out), to_blocks(layer_in), ocean_blocks)))
            stored.append((padded, conv_out, layer_in))
            current = output.astype(jnp.bfloat16)
        flowing = cotangent[replica].astype(jnp.float32) * rescale
        new_kernels = [None] * LAYERS
        new_inner = [None] * LAYERS
        new_outer = [None] * LAYERS
        for layer_index in reversed(range(LAYERS)):
            padded, conv_out, layer_in = stored[layer_index]
            kernel = depth_kernel[replica, layer_index]
            gain_vec = norm_gain[replica, layer_index]
            shift_bias = norm_bias[replica, layer_index]
            weight_in_b = weight_in[replica, layer_index].astype(jnp.bfloat16)
            bias_vec_in = bias_in[replica, layer_index]
            weight_out_b = weight_out[replica, layer_index].astype(jnp.bfloat16)
            bias_vec_out = bias_out[replica, layer_index]
            scale_vec = layer_scale[replica, layer_index]

            def backward_block(running, block_items):
                conv_block, resid_block, ocean_block, grad_block = block_items
                output, kept_values = pointwise_forward(conv_block, resid_block, ocean_block, gain_vec, shift_bias, weight_in_b, bias_vec_in, weight_out_b, bias_vec_out, scale_vec)
                conv_grad, masked, grad_in_w, grad_out_w = pointwise_backward(grad_block, kept_values, ocean_block, gain_vec, weight_in_b, weight_out_b, scale_vec)
                return ((running[0] + grad_in_w, running[1] + grad_out_w), (conv_grad, masked))
            start = (jnp.zeros((channels, HID), jnp.float32), jnp.zeros((HID, channels), jnp.float32))
            grads, pieces = lax.scan(backward_block, start, (to_blocks(conv_out), to_blocks(layer_in), ocean_blocks, to_blocks(flowing)))
            conv_grad = from_blocks(pieces[0])
            res_grad = from_blocks(pieces[1])
            grad_kernel = kernel_grad(padded, conv_grad)
            flowing = res_grad + depthwise(pad_field(conv_grad), kernel[:, ::-1], NX, NY)
            new_kernels[layer_index] = kernel - STEP_RATE * grad_kernel
            new_inner[layer_index] = weight_in[replica, layer_index] - STEP_RATE * grads[0]
            new_outer[layer_index] = weight_out[replica, layer_index] - STEP_RATE * grads[1]
        inner_stack = jnp.stack(new_inner)
        outer_stack = jnp.stack(new_outer)
        kernels_all.append(jnp.stack(new_kernels))
        inner_all.append(inner_stack)
        outer_all.append(outer_stack)
        piece_inner, piece_outer = pick_stretch(anchor_in, anchor_out, inner_stack, outer_stack, choose)
        stretch_inner.append(piece_inner)
        stretch_outer.append(piece_outer)
    cycle_in = jnp.stack([stretch_inner[(replica - 1) % REPS] for replica in range(REPS)])
    cycle_out = jnp.stack([stretch_outer[(replica - 1) % REPS] for replica in range(REPS)])
    return (jnp.stack(kernels_all), jnp.stack(inner_all), jnp.stack(outer_all), cycle_in, cycle_out)
```

```python
import math

import jax
import jax.numpy as jnp
from jax import lax
from jax.experimental import pallas as pl
from jax.experimental.pallas import tpu as pltpu
from jax.sharding import PartitionSpec as P

HID = 768
STRETCHES = 12


EPSILON = 1e-06
STEP_RATE = 0.1
GELU_C = 0.7978845608028654

MESH = pl.DeviceIdType.MESH
XY = 8
EW = 8
TILES = 19
ZT = 3
F32 = jnp.float32
BF16 = jnp.bfloat16


def remote(src, dst, send_sem, recv_sem, device):
    return pltpu.make_async_remote_copy(
        src_ref=src,
        dst_ref=dst,
        send_sem=send_sem,
        recv_sem=recv_sem,
        device_id=device,
        device_id_type=MESH,
    )


def reduce_kernel(
    grads,
    dk,
    total,
    send1,
    recv1,
    own,
    send2,
    recv2,
    send3,
    recv3,
    s1, r1, s2, r2, s3, r3, s4, r4, s5, r5, s6, r6,
):
    rep = lax.axis_index("rep")
    z = lax.axis_index("ew")
    ns = lax.axis_index("ns")
    core = lax.rem(ns, 2)
    chip = ns // 2
    other = 1 - core

    def twin():
        return (rep, z, 2 * chip + other)

    def in_plane(step):
        return (rep, z, 2 * lax.rem(chip + step, XY) + core)

    def on_line(step):
        return (rep, lax.rem(z + step, EW), ns)

    barrier = pltpu.get_barrier_semaphore()
    peers = [twin()] + [in_plane(d) for d in range(1, XY)] + [on_line(d) for d in range(1, EW)]
    for peer in peers:
        pl.semaphore_signal(barrier, inc=1, device_id=peer, device_id_type=MESH)

    def pack(half, dst):
        @pl.loop(0, 2 * 12)
        def _(row):
            layer, block = row // 12, lax.rem(row, 12)
            for col in range(6):
                dst[row * 6 + col] = grads[
                    half, layer, pl.ds(block * 16, 16), 128 * col : 128 * (col + 1)
                ].astype(dst.dtype)

        for block in range(6):
            dst[144 + block] = dk[half, 16 * block : 16 * (block + 1), :].astype(dst.dtype)
        for block in range(150, 152):
            dst[block] = jnp.zeros((16, 128), dst.dtype)

    pack(other, send1)
    pl.semaphore_wait(barrier, len(peers))

    def place(step):
        return pl.ds(TILES * lax.rem(chip + step, XY), TILES)

    first = []
    for step in list(range(1, XY)) + [0]:
        copy = remote(
            send1.at[place(step)], recv1.at[place(step)], s1.at[step], r1.at[step], twin()
        )
        copy.start()
        first.append((step, copy))
    pack(core, own)
    second = []
    for step, copy in first:
        copy.wait_recv()
        part = own[place(step)] + recv1[place(step)].astype(F32)
        if step == 0:
            mine = part
        else:
            send2[step - 1] = part.astype(BF16)
            onward = remote(
                send2.at[step - 1], recv2.at[step - 1], s2.at[step - 1], r2.at[step - 1], in_plane(step)
            )
            onward.start()
            second.append(onward)
    own[pl.ds(0, TILES)] = mine
    send3[...] = jnp.zeros_like(send3)
    for step, copy in enumerate(second):
        copy.wait_recv()
        own[pl.ds(0, TILES)] += recv2[step].astype(F32)
    own[pl.ds(TILES, EW * ZT - TILES)] = jnp.zeros((EW * ZT - TILES, 16, 128), F32)
    send3[pl.ds(0, TILES)] = own[pl.ds(0, TILES)].astype(BF16)

    def stretch(step):
        return pl.ds(ZT * lax.rem(z + step, EW), ZT)

    third = []
    for step in range(1, EW):
        copy = remote(
            send3.at[stretch(step)], recv3.at[step - 1], s3.at[step - 1], r3.at[step - 1], on_line(step)
        )
        copy.start()
        third.append(copy)
    for step, copy in enumerate(third):
        copy.wait_recv()
        own[stretch(0)] += recv3[step].astype(F32)
    here = total.at[core, chip, stretch(0)]
    here[...] = own[stretch(0)].astype(BF16)
    fourth = []
    for step in range(1, EW):
        copy = remote(here, here, s4.at[step - 1], r4.at[step - 1], on_line(step))
        copy.start()
        fourth.append(copy)
    for copy in fourth:
        copy.wait_recv()
    share = total.at[core, chip]
    fifth = []
    for step in range(1, XY):
        copy = remote(share, share, s5.at[step - 1], r5.at[step - 1], in_plane(step))
        copy.start()
        fifth.append(copy)
    sixth = [remote(share, share, s6.at[0], r6.at[0], twin())]
    sixth[0].start()
    for step, copy in enumerate(fifth):
        copy.wait_recv()
        arrived = total.at[core, lax.rem(chip + XY - (step + 1), XY)]
        onward = remote(arrived, arrived, s6.at[step + 1], r6.at[step + 1], twin())
        onward.start()
        sixth.append(onward)
    for copy in sixth:
        copy.wait_recv()
    for _, copy in first:
        copy.wait_send()
    for copy in second + third + fourth + fifth + sixth:
        copy.wait_send()


def summed_over_grid(grads, dk):
    dma = pltpu.SemaphoreType.DMA
    return pl.pallas_call(
        reduce_kernel,
        out_shape=jax.ShapeDtypeStruct((2, XY, EW * ZT, 16, 128), BF16),
        in_specs=[pl.BlockSpec(memory_space=pltpu.VMEM)] * 2,
        out_specs=pl.BlockSpec(memory_space=pltpu.VMEM),
        scratch_shapes=[
            pltpu.VMEM((XY * TILES, 16, 128), BF16),
            pltpu.VMEM((XY * TILES, 16, 128), BF16),
            pltpu.VMEM((XY * TILES, 16, 128), F32),
            pltpu.VMEM((XY - 1, TILES, 16, 128), BF16),
            pltpu.VMEM((XY - 1, TILES, 16, 128), BF16),
            pltpu.VMEM((EW * ZT, 16, 128), BF16),
            pltpu.VMEM((EW - 1, ZT, 16, 128), BF16),
        ]
        + [dma((8,))] * 2 + [dma((7,))] * 8 + [dma((8,))] * 2,
        compiler_params=pltpu.CompilerParams(
            collective_id=0, has_side_effects=True, vmem_limit_bytes=40 * 2**20
        ),
    )(grads, dk)


def unpacked(total):
    flat = total[:, :, :TILES].reshape(2, XY * TILES, 16, 128)
    mats = flat[:, :144].reshape(2, 2, 12, 6, 16, 128).transpose(0, 1, 2, 4, 3, 5)
    mats = mats.reshape(2, 2, 192, 768).astype(F32)
    dk = flat[:, 144:150].reshape(192, 128).astype(F32)
    return mats, dk


def extended(cells, sides, width, closed):
    for axis, dim in sides:
        count = lax.axis_size(axis)
        ends = count if closed else count - 1
        head = lax.slice_in_dim(cells, 0, width, axis=dim)
        tail = lax.slice_in_dim(cells, cells.shape[dim] - width, cells.shape[dim], axis=dim)
        cells = jnp.concatenate(
            [
                lax.ppermute(tail, axis, [(i, (i + 1) % count) for i in range(ends)]),
                cells,
                lax.ppermute(head, axis, [((i + 1) % count, i) for i in range(ends)]),
            ],
            axis=dim,
        )
    return cells


def passed_along(block, axis, distance):
    devices = range(lax.axis_size(axis))
    route = [((i - distance) % len(devices), i) for i in devices]
    return lax.ppermute(block, axis, route)


def depthwise(padded, kernel, extent_x, extent_y):
    summed = jnp.zeros((padded.shape[0], extent_x, extent_y), jnp.float32)
    for tap_row in range(7):
        for tap_col in range(7):
            weight_tap = kernel[:, tap_row * 7 + tap_col][:, None, None]
            summed = (
                summed
                + weight_tap * padded[:, tap_row : tap_row + extent_x, tap_col : tap_col + extent_y]
            )
    return summed


def kernel_grad(padded, conv_grad):
    extent_x = conv_grad.shape[1]
    extent_y = conv_grad.shape[2]
    columns = []
    for tap_row in range(7):
        for tap_col in range(7):
            window = padded[:, tap_row : tap_row + extent_x, tap_col : tap_col + extent_y]
            columns.append(jnp.sum(conv_grad * window, axis=(1, 2)))
    return jnp.stack(columns, axis=1)


def gelu_pair(hidden_pre):
    tanh_arg = GELU_C * (hidden_pre + 0.044715 * hidden_pre * hidden_pre * hidden_pre)
    tanh_val = jnp.tanh(tanh_arg)
    gelu_value = 0.5 * hidden_pre * (1.0 + tanh_val)
    gelu_slope = 0.5 * (1.0 + tanh_val) + 0.5 * hidden_pre * (
        1.0 - tanh_val * tanh_val
    ) * GELU_C * (1.0 + 3.0 * 0.044715 * hidden_pre * hidden_pre)
    return (gelu_value, gelu_slope)


def pointwise_forward(
    conv_out,
    residual,
    ocean_cells,
    gain_vec,
    shift_bias,
    weight_in_b,
    bias_vec_in,
    weight_out_b,
    bias_vec_out,
    scale_vec,
):
    centered = conv_out - jnp.mean(conv_out, axis=0, keepdims=True)
    inv_std = lax.rsqrt(jnp.mean(centered * centered, axis=0, keepdims=True) + EPSILON)
    normed = centered * inv_std
    normed_b = (normed * gain_vec[:, None] + shift_bias[:, None]).astype(jnp.bfloat16)
    hidden_pre = (
        jnp.dot(weight_in_b.T, normed_b, preferred_element_type=jnp.float32) + bias_vec_in[:, None]
    )
    active, gelu_slope = gelu_pair(hidden_pre)
    active_b = active.astype(jnp.bfloat16)
    branch = (
        jnp.dot(weight_out_b.T, active_b, preferred_element_type=jnp.float32)
        + bias_vec_out[:, None]
    )
    output = ocean_cells[None, :] * (residual + scale_vec[:, None] * branch)
    return (output, (normed, inv_std, normed_b, gelu_slope, active_b))


def pointwise_backward(
    flow_grad, kept_values, ocean_cells, gain_vec, weight_in_b, weight_out_b, scale_vec
):
    normed, inv_std, normed_b, gelu_slope, active_b = kept_values
    masked = ocean_cells[None, :] * flow_grad
    branch_grad = (masked * scale_vec[:, None]).astype(jnp.bfloat16)
    grad_out_w = lax.dot_general(
        branch_grad, active_b, (((1,), (1,)), ((), ())), preferred_element_type=jnp.float32
    )
    active_grad = jnp.dot(weight_out_b, branch_grad, preferred_element_type=jnp.float32)
    hidden_grad = (active_grad * gelu_slope).astype(jnp.bfloat16)
    grad_in_w = jnp.dot(normed_b, hidden_grad.T, preferred_element_type=jnp.float32)
    normed_grad = (
        jnp.dot(weight_in_b, hidden_grad, preferred_element_type=jnp.float32) * gain_vec[:, None]
    )
    mean_grad = jnp.mean(normed_grad, axis=0, keepdims=True)
    mean_cross = jnp.mean(normed_grad * normed, axis=0, keepdims=True)
    conv_grad = inv_std * (normed_grad - mean_grad - normed * mean_cross)
    return (conv_grad, masked, grad_in_w, grad_out_w)


def extend_forward(field):
    partial_rim = extended(field, (("ns", 2),), 3, False)
    return extended(partial_rim, (("ew", 1),), 3, True)


def extend_backward(field):
    partial_rim = extended(field.astype(jnp.bfloat16), (("ns", 2),), 3, False).astype(field.dtype)
    return extended(partial_rim.astype(jnp.bfloat16), (("ew", 1),), 3, True).astype(
        partial_rim.dtype
    )


def body(
    fields,
    cotangent,
    land_mask,
    stretch_index,
    depth_kernel,
    norm_gain,
    norm_bias,
    weight_in,
    bias_in,
    weight_out,
    bias_out,
    layer_scale,
    anchor_in,
    anchor_out,
):
    channels = fields.shape[1]
    extent_x = fields.shape[2]
    extent_y = fields.shape[3]
    cell_count = extent_x * extent_y
    layers_count = depth_kernel.shape[1]
    rescale = 1.0 / math.sqrt(extent_x * lax.axis_size("ew") * extent_y * lax.axis_size("ns"))
    ocean_cells = land_mask.astype(jnp.float32).reshape(cell_count)
    current = fields[0]
    stored = []
    for layer_index in range(layers_count):
        padded = extend_forward(current).astype(jnp.float32)
        conv_out = depthwise(padded, depth_kernel[0, layer_index], extent_x, extent_y)
        layer_in = current.astype(jnp.float32).reshape(channels, cell_count)
        output, kept_values = pointwise_forward(
            conv_out.reshape(channels, cell_count),
            layer_in,
            ocean_cells,
            norm_gain[0, layer_index],
            norm_bias[0, layer_index],
            weight_in[0, layer_index].astype(jnp.bfloat16),
            bias_in[0, layer_index],
            weight_out[0, layer_index].astype(jnp.bfloat16),
            bias_out[0, layer_index],
            layer_scale[0, layer_index],
        )
        stored.append((padded, kept_values))
        current = output.reshape(channels, extent_x, extent_y).astype(jnp.bfloat16)
    flowing = cotangent[0].astype(jnp.float32).reshape(channels, cell_count) * rescale
    grads_k = [None] * layers_count
    grads_in = [None] * layers_count
    grads_out = [None] * layers_count
    for layer_index in reversed(range(layers_count)):
        padded, kept_values = stored[layer_index]
        kernel = depth_kernel[0, layer_index]
        conv_grad, masked, grad_in_w, grad_out_w = pointwise_backward(
            flowing,
            kept_values,
            ocean_cells,
            norm_gain[0, layer_index],
            weight_in[0, layer_index].astype(jnp.bfloat16),
            weight_out[0, layer_index].astype(jnp.bfloat16),
            layer_scale[0, layer_index],
        )
        conv_field = conv_grad.reshape(channels, extent_x, extent_y)
        grad_kernel = kernel_grad(padded, conv_field)
        if layer_index > 0:
            spread = extend_backward(conv_field)
            flowing = masked + depthwise(spread, kernel[:, ::-1], extent_x, extent_y).reshape(
                channels, cell_count
            )
        grads_k[layer_index] = grad_kernel
        grads_in[layer_index] = grad_in_w
        grads_out[layer_index] = grad_out_w
    grads = jnp.stack([jnp.stack(grads_in), jnp.stack(grads_out)])
    dk = jnp.concatenate(
        [
            grads_k[0],
            jnp.zeros((channels, 15), F32),
            grads_k[1],
            jnp.zeros((channels, 15), F32),
        ],
        axis=1,
    ).reshape(2, channels // 2, 128)
    mats, dk = unpacked(summed_over_grid(grads, dk))
    new_kernels = [
        depth_kernel[0, 0] - STEP_RATE * dk[:, :49],
        depth_kernel[0, 1] - STEP_RATE * dk[:, 64:113],
    ]
    inner_stack = weight_in[0] - STEP_RATE * mats[0]
    outer_stack = weight_out[0] - STEP_RATE * mats[1].transpose(0, 2, 1)
    choose = stretch_index[0]
    span_width = HID // STRETCHES
    layer_pick = choose // STRETCHES
    start = choose % STRETCHES * span_width
    diff_inner = lax.dynamic_index_in_dim(
        anchor_in, layer_pick, 0, False
    ) - lax.dynamic_index_in_dim(inner_stack, layer_pick, 0, False)
    diff_outer = lax.dynamic_index_in_dim(
        anchor_out, layer_pick, 0, False
    ) - lax.dynamic_index_in_dim(outer_stack, layer_pick, 0, False)
    stretch_inner = lax.dynamic_slice_in_dim(diff_inner, start, span_width, 1)
    stretch_outer = lax.dynamic_slice_in_dim(diff_outer, start, span_width, 0)
    cycle_inner, cycle_outer = passed_along((stretch_inner, stretch_outer), "rep", 1)
    return (
        jnp.stack(new_kernels)[None],
        inner_stack[None],
        outer_stack[None],
        cycle_inner[None],
        cycle_outer[None],
    )


def solution(mesh):
    in_specs = (
        P("rep", None, "ew", "ns"),
        P("rep", None, "ew", "ns"),
        P("ew", "ns"),
        P(),
        P("rep", None, None, None),
        P("rep", None, None),
        P("rep", None, None),
        P("rep", None, None, None),
        P("rep", None, None),
        P("rep", None, None, None),
        P("rep", None, None),
        P("rep", None, None),
        P(),
        P(),
    )
    out_specs = (
        P("rep", None, None, None),
        P("rep", None, None, None),
        P("rep", None, None, None),
        P("rep", None, None),
        P("rep", None, None),
    )
    return jax.shard_map(body, mesh=mesh, in_specs=in_specs, out_specs=out_specs, check_vma=False)
```

```python
import functools

import jax
import jax.numpy as jnp
from jax import lax
from jax.experimental import pallas as pl
from jax.experimental.pallas import tpu as pltpu
from jax.sharding import PartitionSpec as P

EPSILON = 1e-06
STEP_RATE = 0.1
GELU_C = 0.7978845608028654
GELU_D = 0.044715

MESH = pl.DeviceIdType.MESH
F32 = jnp.float32
BF16 = jnp.bfloat16
C = 192
HID = 768
LAYERS = 2
CX = 4
CY = 128
CELLS = CX * CY
ROWS = CX + 6
BLOCKS = C // 8
FOLD = 4
FOLDED = C // FOLD
XY = 8
EW = 8
NS = 16
ZT = 2
GAIN, SHIFT, OUT_BIAS, SCALE = 49, 50, 51, 52
SHARES = (10, 9)


def remote(src, dst, send_sem, recv_sem, device):
    return pltpu.make_async_remote_copy(
        src_ref=src,
        dst_ref=dst,
        send_sem=send_sem,
        recv_sem=recv_sem,
        device_id=device,
        device_id_type=MESH,
    )


def lanes_of(shape):
    return lax.broadcasted_iota(jnp.int32, shape, 1)


def dot(left, right):
    return jnp.dot(left, right, preferred_element_type=F32)


def dot_cells(left, right):
    return lax.dot_general(left, right, (((1,), (1,)), ((), ())), preferred_element_type=F32)


def rounded(cells):
    return cells.astype(BF16).astype(F32)


class Place:
    def __init__(self):
        self.rep = lax.axis_index("rep")
        self.z = lax.axis_index("ew")
        self.ns = lax.axis_index("ns")
        self.core = lax.rem(self.ns, 2)
        self.chip = self.ns // 2

    def twin(self):
        return (self.rep, self.z, 2 * self.chip + 1 - self.core)

    def in_plane(self, step):
        return (self.rep, self.z, 2 * lax.rem(self.chip + step, XY) + self.core)

    def on_line(self, step):
        return (self.rep, lax.rem(self.z + step, EW), self.ns)

    def beside(self, step_z, step_ns):
        return (
            self.rep,
            lax.rem(self.z + EW + step_z, EW),
            lax.rem(self.ns + NS + step_ns, NS),
        )


AROUND = [(dz, dn) for dn in (1, -1) for dz in (-1, 0, 1)]


class Halo:
    def __init__(self, place, turn, out_rows, out_edges, in_rows, in_edges, sent, came):
        self.place = place
        self.out_rows = out_rows.at[turn]
        self.out_edges = out_edges.at[turn]
        self.in_rows = in_rows.at[turn]
        self.in_edges = in_edges.at[turn]
        self.sent = sent.at[turn]
        self.came = came.at[turn]
        self.copies = []

    def start(self, source):
        lane = lanes_of((FOLDED, CY))
        group = lane // 32
        inside = lane % 32
        folded = jnp.zeros((FOLDED, CY), F32)
        for x in range(CX):
            row = source(x)
            self.out_rows[x] = row.astype(BF16)
            for part in range(FOLD):
                piece = row[FOLDED * part : FOLDED * (part + 1), :]
                base = 32 * part + 8 * x
                low = pltpu.roll(piece, base, 1) if base else piece
                high = pltpu.roll(piece, (base + 8) % CY, 1) if (base + 8) % CY else piece
                here = group == part
                folded = jnp.where(here & (inside >= 8 * x) & (inside < 8 * x + 3), low, folded)
                folded = jnp.where(here & (inside >= 8 * x + 5) & (inside < 8 * x + 8), high, folded)
        self.out_edges[...] = folded.astype(BF16)
        place = self.place
        rows = [
            remote(
                self.out_rows.at[pl.ds(1, 3)],
                self.in_rows.at[0],
                self.sent.at[0],
                self.came.at[0],
                place.beside(1, 0),
            ),
            remote(
                self.out_rows.at[pl.ds(0, 3)],
                self.in_rows.at[1],
                self.sent.at[1],
                self.came.at[1],
                place.beside(-1, 0),
            ),
        ]
        edges = []
        for number, (dz, dn) in enumerate(AROUND):
            side = 0 if dn == 1 else 1
            edges.append(
                remote(
                    self.out_edges,
                    self.in_edges.at[side, 1 - dz],
                    self.sent.at[2 + number],
                    self.came.at[2 + number],
                    place.beside(dz, dn),
                )
            )
        self.copies = edges + rows
        for copy in self.copies:
            copy.start()

    def finish(self, main, halo):
        for copy in self.copies:
            copy.wait_recv()
        for row in range(3):
            main[row] = self.in_rows[0, row].astype(F32)
            main[CX + 3 + row] = self.in_rows[1, row].astype(F32)
        keep_left = (self.place.ns > 0).astype(F32)
        keep_right = (self.place.ns < NS - 1).astype(F32)
        lane = lanes_of((FOLDED, CY))
        for index in range(3):
            left = self.in_edges[0, index].astype(F32) * keep_left
            right = self.in_edges[1, index].astype(F32) * keep_right
            for x in range(CX):
                row = (x - 1, x + 3, x + 7)[index]
                if (index == 0 and x == 0) or (index == 2 and x == 3):
                    continue
                for part in range(FOLD):
                    base = 32 * part + 8 * x
                    from_left = pltpu.roll(left, (120 - base) % CY, 1) if base != 120 else left
                    from_right = pltpu.roll(right, (CY - base) % CY, 1) if base else right
                    halo[row, FOLDED * part : FOLDED * (part + 1), :] = jnp.where(
                        lane < 64, from_right, from_left
                    )

    def close(self):
        for copy in self.copies:
            copy.wait_send()


def shifted(main, halo, distance, lane):
    if distance == 0:
        return main
    if distance > 0:
        chosen = jnp.where(lane < distance, halo, main)
    else:
        chosen = jnp.where(lane >= CY + distance, halo, main)
    return pltpu.roll(chosen, (-distance) % CY, 1)


def depthwise(main, halo, taps, out, keep, reverse):
    @pl.loop(0, BLOCKS)
    def _(block):
        at = pl.ds(block * 8, 8)
        lane = lanes_of((8, CY))
        weights = taps[at, :]
        total = [jnp.zeros((8, CY), F32) for _ in range(CX)]
        for col in range(7):
            rows = []
            for row in range(ROWS):
                moved = shifted(main[row, at, :], halo[row, at, :], col - 3, lane)
                if keep is not None and col != 3:
                    keep[col, row, at, :] = moved
                rows.append(moved)
            for tap_row in range(7):
                tap = 7 * tap_row + col
                if reverse:
                    tap = 48 - tap
                weight = jnp.broadcast_to(weights[:, tap : tap + 1], (8, CY))
                for x in range(CX):
                    total[x] = total[x] + weight * rows[x + tap_row]
        for x in range(CX):
            out[x, at, :] = total[x]


def kernel_grad(windows, conv_grad, out, lane_base, first):
    @pl.loop(0, BLOCKS)
    def _(block):
        at = pl.ds(block * 8, 8)
        lane = lanes_of((8, CY))
        grads = [conv_grad[x, at, :] for x in range(CX)]
        result = jnp.zeros((8, CY), F32)
        for col in range(7):
            rows = [windows[col, row, at, :] for row in range(ROWS)]
            for tap_row in range(7):
                total = grads[0] * rows[tap_row]
                for x in range(1, CX):
                    total = total + grads[x] * rows[x + tap_row]
                tap = 7 * tap_row + col
                result = jnp.where(
                    lane == tap + lane_base, jnp.sum(total, axis=1, keepdims=True), result
                )
        if first:
            out[at, :] = result
        else:
            out[at, :] = out[at, :] + result


class Sum:
    def __init__(self, place, tiles, send1, recv1, own, send2, recv2, send3, recv3, total, sems):
        self.place = place
        self.tiles = tiles
        self.send1, self.recv1, self.own = send1, recv1, own
        self.send2, self.recv2, self.send3, self.recv3 = send2, recv2, send3, recv3
        self.total = total
        self.sems = sems
        self.started = []

    def go(self, copy):
        copy.start()
        self.started.append(copy)
        return copy

    def pair(self, phase, step):
        return self.sems[2 * phase].at[step], self.sems[2 * phase + 1].at[step]

    def pack(self, grads, extra, half, dst):
        @pl.loop(0, 12)
        def _(row):
            for col in range(6):
                dst[row * 6 + col] = grads[
                    half, pl.ds(row * 16, 16), 128 * col : 128 * (col + 1)
                ].astype(dst.dtype)

        if extra is not None:
            for block in range(6):
                dst[72 + block] = extra[pl.ds(half * 96 + 16 * block, 16), :].astype(dst.dtype)
            dst[pl.ds(78, 2)] = jnp.zeros((2, 16, 128), dst.dtype)

    def share(self, step):
        return pl.ds(self.tiles * lax.rem(self.place.chip + step, XY), self.tiles)

    def start(self, grads, extra):
        core = self.place.core
        self.pack(grads, extra, 1 - core, self.send1)
        self.first = []
        for step in list(range(1, XY)) + [0]:
            part = self.share(step)
            copy = remote(
                self.send1.at[part], self.recv1.at[part], *self.pair(0, step), self.place.twin()
            )
            self.first.append((step, self.go(copy)))
        self.pack(grads, extra, core, self.own)

    def to_plane(self):
        self.second = []
        for step, copy in self.first:
            copy.wait_recv()
            part = self.own[self.share(step)] + self.recv1[self.share(step)].astype(F32)
            if step == 0:
                self.own[pl.ds(0, self.tiles)] = part
            else:
                self.send2[step - 1] = part.astype(BF16)
                copy = remote(
                    self.send2.at[step - 1],
                    self.recv2.at[step - 1],
                    *self.pair(1, step - 1),
                    self.place.in_plane(step),
                )
                self.second.append(self.go(copy))

    def stretch(self, step):
        return pl.ds(ZT * lax.rem(self.place.z + step, EW), ZT)

    def to_line(self):
        own = pl.ds(0, self.tiles)
        for copy in self.second:
            copy.wait_recv()
        part = self.own[own]
        for step in range(XY - 1):
            part = part + self.recv2[step].astype(F32)
        self.own[own] = part
        rest = pl.ds(self.tiles, EW * ZT - self.tiles)
        self.own[rest] = jnp.zeros((EW * ZT - self.tiles, 16, 128), F32)
        self.send3[pl.ds(0, EW * ZT)] = self.own[pl.ds(0, EW * ZT)].astype(BF16)
        self.third = []
        for step in range(1, EW):
            copy = remote(
                self.send3.at[self.stretch(step)],
                self.recv3.at[step - 1],
                *self.pair(2, step - 1),
                self.place.on_line(step),
            )
            self.third.append(self.go(copy))

    def back_line(self):
        for copy in self.third:
            copy.wait_recv()
        part = self.own[self.stretch(0)]
        for step in range(EW - 1):
            part = part + self.recv3[step].astype(F32)
        here = self.total.at[self.place.core, self.place.chip, self.stretch(0)]
        here[...] = part.astype(BF16)
        self.fourth = []
        for step in range(1, EW):
            copy = remote(here, here, *self.pair(3, step - 1), self.place.on_line(step))
            self.fourth.append(self.go(copy))

    def back_plane(self):
        for copy in self.fourth:
            copy.wait_recv()
        mine = self.total.at[self.place.core, self.place.chip]
        self.fifth = []
        for step in range(1, XY):
            copy = remote(mine, mine, *self.pair(4, step - 1), self.place.in_plane(step))
            self.fifth.append(self.go(copy))
        self.sixth = [self.go(remote(mine, mine, *self.pair(5, 0), self.place.twin()))]

    def back_twin(self):
        for step, copy in enumerate(self.fifth):
            copy.wait_recv()
            came = self.total.at[
                self.place.core, lax.rem(self.place.chip + XY - (step + 1), XY)
            ]
            copy = remote(came, came, *self.pair(5, step + 1), self.place.twin())
            self.sixth.append(self.go(copy))
        for copy in self.sixth:
            copy.wait_recv()

    def close(self):
        for copy in self.started:
            copy.wait_send()


def step_kernel(
    x_in,
    cot_in,
    mask_in,
    rows_in,
    bias_in,
    win,
    wout_t,
    total0,
    total1,
    cols,
    bias_col,
    win_b,
    win_tb,
    wout_tb,
    wout_b,
    windows,
    halo,
    conv,
    normed,
    inv_std,
    norm_b,
    hidden,
    slope,
    act_b,
    flow,
    back_b,
    hid_b,
    conv_grad,
    grad_w,
    grad_k,
    out_rows,
    out_edges,
    in_rows,
    in_edges,
    send1,
    recv1,
    own,
    send2,
    recv2,
    send3,
    recv3,
    halo_sent,
    halo_came,
    *sems,
):
    place = Place()
    barrier = pltpu.get_barrier_semaphore()
    peers = [place.twin()]
    peers += [place.in_plane(d) for d in range(1, XY)]
    peers += [place.on_line(d) for d in range(1, EW)]
    peers += [place.beside(dz, dn) for dz, dn in AROUND]
    for peer in peers:
        pl.semaphore_signal(barrier, inc=1, device_id=peer, device_id_type=MESH)

    def lanes(x):
        return slice(CY * x, CY * (x + 1))

    for layer in range(LAYERS):
        cols[layer] = rows_in[layer].T[:C]
        win_b[layer] = win[layer].astype(BF16)
        win_tb[layer] = win[layer].T.astype(BF16)
        wout_tb[layer] = wout_t[layer].astype(BF16)
        wout_b[layer] = wout_t[layer].T.astype(BF16)
    bias_col[...] = bias_in[...].T
    pl.semaphore_wait(barrier, len(peers))

    halos = [
        Halo(place, turn, out_rows, out_edges, in_rows, in_edges, halo_sent, halo_came)
        for turn in range(3)
    ]
    sums = [
        Sum(
            place,
            SHARES[layer],
            send1.at[layer],
            recv1.at[layer],
            own.at[layer],
            send2.at[layer, :, pl.ds(0, SHARES[layer])],
            recv2.at[layer, :, pl.ds(0, SHARES[layer])],
            send3.at[layer],
            recv3.at[layer],
            (total0, total1)[layer],
            sems[12 * layer : 12 * (layer + 1)],
        )
        for layer in range(LAYERS)
    ]

    ocean = [mask_in[x : x + 1, :].astype(F32) for x in range(CX)]

    def column(layer, which):
        return cols[layer, :, which : which + 1]

    def forward(layer):
        main = windows.at[layer, 3]
        halos[layer].finish(main, halo)
        depthwise(main, halo, cols.at[layer], conv, windows.at[layer], False)
        for x in range(CX):
            cells = conv[x]
            centered = cells - jnp.mean(cells, axis=0, keepdims=True)
            inv = lax.rsqrt(jnp.mean(centered * centered, axis=0, keepdims=True) + EPSILON)
            unit = centered * inv
            inv_std[layer, x : x + 1, :] = inv
            normed[layer, x] = unit
            norm_b[layer, :, lanes(x)] = (
                unit * column(layer, GAIN) + column(layer, SHIFT)
            ).astype(BF16)
        hidden[...] = dot(win_tb[layer], norm_b[layer])

        @pl.loop(0, HID // 16)
        def _(block):
            at = pl.ds(block * 16, 16)
            pre = hidden[at, :] + bias_col[at, layer : layer + 1]
            square = pre * pre
            bend = GELU_C * GELU_D * square
            gate = 0.5 + 0.5 * jnp.tanh(pre * (GELU_C + bend))
            value = pre * gate
            act_b[layer, at, :] = value.astype(BF16)
            slope[layer, at, :] = gate + 2.0 * value * (1.0 - gate) * (GELU_C + 3.0 * bend)

    def output(layer):
        branch = dot(wout_tb[layer], act_b[layer])
        for x in range(CX):
            inner = branch[:, lanes(x)] + column(layer, OUT_BIAS)
            value = ocean[x] * (windows[layer, 3, 3 + x] + column(layer, SCALE) * inner)
            windows[layer + 1, 3, 3 + x] = rounded(value)

    def backward(layer):
        for x in range(CX):
            masked = ocean[x] * flow[x]
            flow[x] = masked
            back_b[:, lanes(x)] = (masked * column(layer, SCALE)).astype(BF16)
        grad_w[layer, 1] = dot_cells(back_b[...], act_b[layer])
        hidden[...] = dot(wout_b[layer], back_b[...])

        @pl.loop(0, HID // 16)
        def _(block):
            at = pl.ds(block * 16, 16)
            hid_b[at, :] = (hidden[at, :] * slope[layer, at, :]).astype(BF16)

        grad_w[layer, 0] = dot_cells(norm_b[layer], hid_b[...])
        norm_grad = dot(win_b[layer], hid_b[...])
        for x in range(CX):
            part = norm_grad[:, lanes(x)] * column(layer, GAIN)
            unit = normed[layer, x]
            mean_grad = jnp.mean(part, axis=0, keepdims=True)
            mean_cross = jnp.mean(part * unit, axis=0, keepdims=True)
            conv_grad[x] = inv_std[layer, x : x + 1, :] * (part - mean_grad - unit * mean_cross)

    for x in range(CX):
        windows[0, 3, 3 + x] = x_in[x].astype(F32)
    halos[0].start(lambda x: windows[0, 3, 3 + x])
    forward(0)
    output(0)
    halos[1].start(lambda x: windows[1, 3, 3 + x])
    for x in range(CX):
        flow[x] = cot_in[x].astype(F32) * (1.0 / 256.0)
    forward(1)
    backward(1)
    halos[2].start(lambda x: conv_grad[x])
    sums[1].start(grad_w.at[1], None)
    kernel_grad(windows.at[1], conv_grad, grad_k, 64, True)
    sums[1].to_plane()
    main = windows.at[1, 3]
    for x in range(CX):
        main[3 + x] = conv_grad[x]
    halos[2].finish(main, halo)
    depthwise(main, halo, cols.at[1], conv, None, True)
    for x in range(CX):
        flow[x] = flow[x] + conv[x]
    sums[1].to_line()
    backward(0)
    sums[1].back_line()
    kernel_grad(windows.at[0], conv_grad, grad_k, 0, False)
    sums[0].start(grad_w.at[0], grad_k)
    sums[1].back_plane()
    sums[0].to_plane()
    sums[1].back_twin()
    sums[0].to_line()
    sums[0].back_line()
    sums[0].back_plane()
    sums[0].back_twin()
    for each in halos + sums:
        each.close()


def whole_step(x, cot, mask, rows, bias, win, wout_t):
    dma = pltpu.SemaphoreType.DMA
    vmem = pltpu.VMEM
    tiles = XY * max(SHARES)
    total = jax.ShapeDtypeStruct((2, XY, EW * ZT, 16, 128), BF16)
    sums = ([dma((8,))] * 2 + [dma((7,))] * 8 + [dma((8,))] * 2) * LAYERS
    return pl.pallas_call(
        step_kernel,
        out_shape=[total, total],
        in_specs=[pl.BlockSpec(memory_space=pltpu.VMEM)] * 7,
        out_specs=[pl.BlockSpec(memory_space=pltpu.VMEM)] * 2,
        scratch_shapes=[
            vmem((LAYERS, C, 128), F32),
            vmem((HID, 128), F32),
            vmem((LAYERS, C, HID), BF16),
            vmem((LAYERS, HID, C), BF16),
            vmem((LAYERS, C, HID), BF16),
            vmem((LAYERS, HID, C), BF16),
            vmem((LAYERS, 7, ROWS, C, CY), F32),
            vmem((ROWS, C, CY), F32),
            vmem((CX, C, CY), F32),
            vmem((LAYERS, CX, C, CY), F32),
            vmem((LAYERS, CX, CY), F32),
            vmem((LAYERS, C, CELLS), BF16),
            vmem((HID, CELLS), F32),
            vmem((LAYERS, HID, CELLS), F32),
            vmem((LAYERS, HID, CELLS), BF16),
            vmem((CX, C, CY), F32),
            vmem((C, CELLS), BF16),
            vmem((HID, CELLS), BF16),
            vmem((CX, C, CY), F32),
            vmem((LAYERS, 2, C, HID), F32),
            vmem((C, 128), F32),
            vmem((3, CX, C, CY), BF16),
            vmem((3, FOLDED, CY), BF16),
            vmem((3, 2, 3, C, CY), BF16),
            vmem((3, 2, 3, FOLDED, CY), BF16),
            vmem((LAYERS, tiles, 16, 128), BF16),
            vmem((LAYERS, tiles, 16, 128), BF16),
            vmem((LAYERS, tiles, 16, 128), F32),
            vmem((LAYERS, XY - 1, max(SHARES), 16, 128), BF16),
            vmem((LAYERS, XY - 1, max(SHARES), 16, 128), BF16),
            vmem((LAYERS, EW * ZT, 16, 128), BF16),
            vmem((LAYERS, EW - 1, ZT, 16, 128), BF16),
            dma((3, 8)),
            dma((3, 8)),
        ]
        + sums,
        compiler_params=pltpu.CompilerParams(
            collective_id=0, has_side_effects=True, vmem_limit_bytes=56 * 2**20
        ),
    )(x, cot, mask, rows, bias, win, wout_t)


def update_kernel(
    index, total0, total1, win, wout_t, anchor_in, anchor_out, kernel, new_in, new_out, new_k, cycle
):
    for layer, total in enumerate((total0, total1)):
        tiles = SHARES[layer]
        for tile in range(72):
            row, col = tile // 6, tile % 6
            at = (layer, slice(16 * row, 16 * (row + 1)), slice(128 * col, 128 * (col + 1)))
            spot = (tile // tiles, tile % tiles)
            new_in[at] = win[at] - STEP_RATE * total[(0,) + spot].astype(F32)
            new_out[at] = wout_t[at] - STEP_RATE * total[(1,) + spot].astype(F32)
    tiles = SHARES[0]
    grads = []
    for half in range(2):
        for block in range(6):
            tile = 72 + block
            grads.append(total0[half, tile // tiles, tile % tiles].astype(F32))
    taps = jnp.concatenate(grads, axis=0).T
    for layer in range(LAYERS):
        new_k[layer] = kernel[layer] - STEP_RATE * taps[64 * layer : 64 * layer + 49, :]
    layer = index[0] // 12
    within = lax.rem(index[0], 12)
    block = pl.ds(pl.multiple_of(within // 2 * 128, 128), 128)
    odd = lax.rem(within, 2) == 1
    first = anchor_in[layer, :, block] - new_in[layer, :, block]
    second = anchor_out[layer, :, block] - new_out[layer, :, block]
    turned = pltpu.roll(first, 64, 1)
    first = jnp.where(odd, turned, first)
    turned = pltpu.roll(second, 64, 1)
    second = jnp.where(odd, second, turned)
    lane = lanes_of((C, 128))
    cycle[...] = jnp.where(lane < 64, first, second).T


def update(index, total0, total1, win, wout_t, anchor_in, anchor_out, kernel):
    weights = jax.ShapeDtypeStruct((LAYERS, C, HID), F32)
    return pl.pallas_call(
        update_kernel,
        out_shape=[
            weights,
            weights,
            jax.ShapeDtypeStruct((LAYERS, 49, C), F32),
            jax.ShapeDtypeStruct((128, C), F32),
        ],
        in_specs=[pl.BlockSpec(memory_space=pltpu.SMEM)]
        + [pl.BlockSpec(memory_space=pltpu.VMEM)] * 7,
        out_specs=[pl.BlockSpec(memory_space=pltpu.VMEM)] * 4,
        compiler_params=pltpu.CompilerParams(vmem_limit_bytes=40 * 2**20),
    )(index, total0, total1, win, wout_t, anchor_in, anchor_out, kernel)


def body(
    fields,
    cotangent,
    land_mask,
    stretch_index,
    depth_kernel,
    norm_gain,
    norm_bias,
    weight_in,
    bias_in,
    weight_out,
    bias_out,
    layer_scale,
    anchor_in,
    anchor_out,
):
    x = fields[0].transpose(1, 0, 2)
    cot = cotangent[0].transpose(1, 0, 2)
    taps = depth_kernel[0].transpose(0, 2, 1)
    vectors = jnp.stack([norm_gain[0], norm_bias[0], bias_out[0], layer_scale[0]], axis=1)
    rows = jnp.concatenate([taps, vectors], axis=1)
    rows = jnp.pad(rows, ((0, 0), (0, 128 - rows.shape[1]), (0, 256 - C)))
    bias = jnp.pad(bias_in[0], ((0, 128 - LAYERS), (0, 0)))
    win = weight_in[0]
    wout_t = weight_out[0].transpose(0, 2, 1)
    total0, total1 = whole_step(x, cot, land_mask, rows, bias, win, wout_t)
    new_in, new_out, new_k, cycle = update(
        stretch_index,
        total0,
        total1,
        win,
        wout_t,
        anchor_in,
        anchor_out.transpose(0, 2, 1),
        taps,
    )
    cycle = lax.ppermute(cycle, "rep", [(0, 1), (1, 0)])
    return (
        new_k.transpose(0, 2, 1)[None],
        new_in[None],
        new_out.transpose(0, 2, 1)[None],
        cycle[:64].T[None],
        cycle[64:][None],
    )


def solution(mesh):
    in_specs = (
        P("rep", None, "ew", "ns"),
        P("rep", None, "ew", "ns"),
        P("ew", "ns"),
        P(),
        P("rep", None, None, None),
        P("rep", None, None),
        P("rep", None, None),
        P("rep", None, None, None),
        P("rep", None, None),
        P("rep", None, None, None),
        P("rep", None, None),
        P("rep", None, None),
        P(),
        P(),
    )
    out_specs = (
        P("rep", None, None, None),
        P("rep", None, None, None),
        P("rep", None, None, None),
        P("rep", None, None),
        P("rep", None, None),
    )
    return jax.shard_map(body, mesh=mesh, in_specs=in_specs, out_specs=out_specs, check_vma=False)
```

```python
import jax
import jax.numpy as jnp
from jax import lax
from jax.experimental import pallas as pl
from jax.experimental.pallas import tpu as pltpu
from jax.sharding import PartitionSpec as P

EPSILON = 1e-06
STEP_RATE = 0.1
GELU_C = 0.7978845608028654
GELU_D = 0.044715

MESH = pl.DeviceIdType.MESH
F32 = jnp.float32
BF16 = jnp.bfloat16
C = 192
HID = 768
LAYERS = 2
CX = 4
CY = 128
CELLS = CX * CY
ROWS = CX + 6
BLOCKS = C // 8
FOLD = 4
FOLDED = C // FOLD
XY = 8
EW = 8
SHIFTED = (0, 1, 2, 4, 5, 6)
NS = 16
ZT = 2
GAIN, SHIFT, OUT_BIAS, SCALE = 49, 50, 51, 52
SHARE = 9
MAIN = 3 * ROWS + 3
SHARES = (10, 9)


def remote(src, dst, send_sem, recv_sem, device):
    return pltpu.make_async_remote_copy(
        src_ref=src,
        dst_ref=dst,
        send_sem=send_sem,
        recv_sem=recv_sem,
        device_id=device,
        device_id_type=MESH,
    )


def lanes_of(shape):
    return lax.broadcasted_iota(jnp.int32, shape, 1)


def dot(left, right):
    return jnp.dot(left, right, preferred_element_type=F32)


def dot_cells(left, right):
    return lax.dot_general(left, right, (((1,), (1,)), ((), ())), preferred_element_type=F32)


class Place:
    def __init__(self):
        self.rep = lax.axis_index("rep")
        self.z = lax.axis_index("ew")
        self.ns = lax.axis_index("ns")
        self.core = lax.rem(self.ns, 2)
        self.chip = self.ns // 2

    def twin(self):
        return (self.rep, self.z, 2 * self.chip + 1 - self.core)

    def in_plane(self, step):
        return (self.rep, self.z, 2 * lax.rem(self.chip + step, XY) + self.core)

    def on_line(self, step):
        return (self.rep, lax.rem(self.z + step, EW), self.ns)

    def beside(self, step_z, step_ns):
        return (
            self.rep,
            lax.rem(self.z + EW + step_z, EW),
            lax.rem(self.ns + NS + step_ns, NS),
        )


AROUND = [(dz, dn) for dn in (1, -1) for dz in (-1, 0, 1)]


class Halo:
    def __init__(self, place, turn, rows, out_edges, in_rows, in_edges, sent, came):
        self.place = place
        self.rows = rows
        self.out_edges = out_edges.at[turn]
        self.in_rows = in_rows.at[turn]
        self.in_edges = in_edges.at[turn]
        self.sent = sent.at[turn]
        self.came = came.at[turn]
        self.row_copies = []
        self.edge_copies = []

    def start(self):
        place = self.place
        for number, (first, step) in enumerate(((1, 1), (0, -1))):
            copy = remote(
                self.rows.at[pl.ds(first, 3)],
                self.in_rows.at[number],
                self.sent.at[number],
                self.came.at[number],
                place.beside(step, 0),
            )
            copy.start()
            self.row_copies.append(copy)
        slot = ((lanes_of((FOLDED, CY)) + 4) % CY) // 8
        folded = jnp.zeros((FOLDED, CY), F32)
        for x in range(CX):
            row = self.rows[x].astype(F32)
            for part in range(FOLD):
                piece = row[FOLDED * part : FOLDED * (part + 1), :]
                number = 4 * part + x
                moved = pltpu.roll(piece, 8 * number, 1) if number else piece
                folded = jnp.where(slot == number, moved, folded)
        self.out_edges[...] = folded.astype(BF16)
        for number, (dz, dn) in enumerate(AROUND):
            side = 0 if dn == 1 else 1
            copy = remote(
                self.out_edges,
                self.in_edges.at[side, 1 - dz],
                self.sent.at[2 + number],
                self.came.at[2 + number],
                place.beside(dz, dn),
            )
            copy.start()
            self.edge_copies.append(copy)

    def near(self, shifts, halo, windows):
        for copy in self.edge_copies:
            copy.wait_recv()
        keep_left = (self.place.ns > 0).astype(F32)
        keep_right = (self.place.ns < NS - 1).astype(F32)
        low = (lanes_of((FOLDED, CY)) + 4) % 8 < 4
        for index in range(3):
            edges = jnp.where(
                low,
                self.in_edges[0, index].astype(F32) * keep_left,
                self.in_edges[1, index].astype(F32) * keep_right,
            )
            for x in range(CX):
                row = (x - 1, x + 3, x + 7)[index]
                if (index == 0 and x == 0) or (index == 2 and x == 3):
                    continue
                for part in range(FOLD):
                    number = 4 * part + x
                    moved = pltpu.roll(edges, CY - 8 * number, 1) if number else edges
                    halo[row, FOLDED * part : FOLDED * (part + 1), :] = moved.astype(BF16)

        self.shift(self.rows, 3, CX, shifts, halo, windows)

    def shift(self, rows, first, count, shifts, halo, windows):
        cells = jnp.concatenate(
            [
                rows[...].reshape(count * C, CY),
                halo[first : first + count].reshape(count * C, CY),
            ],
            axis=1,
        )
        moved = dot(cells, shifts[...])
        for place, col in enumerate(SHIFTED):
            start = col * ROWS + first
            windows[start : start + count] = moved[:, CY * place : CY * (place + 1)].reshape(
                count, C, CY
            )

    def far(self, shifts, halo, windows):
        for copy in self.row_copies:
            copy.wait_recv()
        for side, first in ((0, 0), (1, CX + 3)):
            self.shift(self.in_rows.at[side], first, 3, shifts, halo, windows)
            start = 3 * ROWS + first
            windows[start : start + 3] = self.in_rows[side].astype(F32)

    def close(self):
        for copy in self.row_copies + self.edge_copies:
            copy.wait_send()


def shift_matrix():
    source = lax.broadcasted_iota(jnp.int32, (2 * CY, CY), 0)
    lane = lanes_of((2 * CY, CY))
    parts = []
    for col in SHIFTED:
        wanted = lane + (col - 3)
        hit = (source == wanted) | (source == wanted + 2 * CY)
        parts.append(hit.astype(F32).astype(BF16))
    return jnp.concatenate(parts, axis=1)


def spread_taps(taps, out):
    @pl.loop(0, BLOCKS, unroll=4)
    def _(block):
        at = pl.ds(block * 8, 8)
        weights = taps[at, :]
        for tap in range(49):
            out[tap, at, :] = jnp.broadcast_to(weights[:, tap : tap + 1], (8, CY))


def depthwise(windows, spread, out, reverse, own):
    @pl.loop(0, BLOCKS, unroll=2)
    def _(block):
        at = pl.ds(block * 8, 8)
        total = [None if own else out[x, at, :] for x in range(CX)]
        used = [row for row in range(ROWS) if (3 <= row < 3 + CX) == own]
        for col in range(7):
            rows = {row: windows[col * ROWS + row, at, :] for row in used}
            part = [None] * CX
            for tap_row in range(7):
                if not any(x + tap_row in rows for x in range(CX)):
                    continue
                tap = 7 * tap_row + col
                weight = spread[48 - tap if reverse else tap, at, :]
                for x in range(CX):
                    if x + tap_row in rows:
                        term = weight * rows[x + tap_row]
                        part[x] = term if part[x] is None else part[x] + term
            for x in range(CX):
                if part[x] is not None:
                    total[x] = part[x] if total[x] is None else total[x] + part[x]
        for x in range(CX):
            out[x, at, :] = total[x]


def kernel_grad(windows, conv_grad, out, lane_base, first):
    @pl.loop(0, BLOCKS, unroll=4)
    def _(block):
        at = pl.ds(block * 8, 8)
        lane = lanes_of((8, CY))
        grads = [conv_grad[x, at, :] for x in range(CX)]
        result = jnp.zeros((8, CY), F32)
        for col in range(7):
            rows = [windows[col * ROWS + row, at, :] for row in range(ROWS)]
            for tap_row in range(7):
                total = grads[0] * rows[tap_row]
                for x in range(1, CX):
                    total = total + grads[x] * rows[x + tap_row]
                tap = 7 * tap_row + col
                result = jnp.where(
                    lane == tap + lane_base, jnp.sum(total, axis=1, keepdims=True), result
                )
        if first:
            out[at, :] = result
        else:
            out[at, :] = out[at, :] + result


class Sum:
    def __init__(
        self, place, tiles, send1, recv1, own, mine, send2, recv2, send3, recv3, line, total, sems
    ):
        self.place = place
        self.tiles = tiles
        self.send1, self.recv1, self.own, self.mine = send1, recv1, own, mine
        self.send2, self.recv2, self.send3, self.recv3 = send2, recv2, send3, recv3
        self.line = line
        self.total = total
        self.sems = sems
        self.started = []
        self.extra = None

    def go(self, copy):
        copy.start()
        self.started.append(copy)
        return copy

    def pair(self, phase, step):
        return self.sems[2 * phase].at[step], self.sems[2 * phase + 1].at[step]

    def pack(self, grads, half, dst):
        @pl.loop(0, 12, unroll=2)
        def _(row):
            for col in range(6):
                dst[row * 6 + col] = grads[
                    half, pl.ds(row * 16, 16), 128 * col : 128 * (col + 1)
                ].astype(dst.dtype)

    def pack_extra(self, extra, half, dst):
        for block in range(6):
            dst[72 + block] = extra[pl.ds(half * 96 + 16 * block, 16), :].astype(dst.dtype)
        dst[78:80] = jnp.zeros((2, 16, 128), dst.dtype)

    def chunk(self, step):
        return lax.rem(self.place.chip + step, XY)

    def share(self, step):
        return pl.ds(SHARE * self.chunk(step), SHARE)

    def start(self, grads):
        core = self.place.core
        self.pack(grads, 1 - core, self.send1)
        self.first = []
        for step in list(range(1, XY)) + [0]:
            part = self.share(step)
            copy = remote(
                self.send1.at[part], self.recv1.at[part], *self.pair(0, step), self.place.twin()
            )
            self.first.append((step, self.go(copy)))
        self.pack(grads, core, self.own)

    def start_extra(self, extra):
        core = self.place.core
        self.pack_extra(extra, 1 - core, self.send1)
        part = pl.ds(72, 8)
        self.extra = self.go(
            remote(self.send1.at[part], self.recv1.at[part], *self.pair(0, 8), self.place.twin())
        )
        self.pack_extra(extra, core, self.own)

    def to_plane(self):
        self.second = []
        if self.extra is not None:
            self.extra.wait_recv()
        self.mine[...] = jnp.zeros_like(self.mine)
        for step, copy in self.first:
            copy.wait_recv()
            part = self.own[self.share(step)] + self.recv1[self.share(step)].astype(F32)
            if self.extra is not None:
                spot = 72 + self.chunk(step)
                more = self.own[spot] + self.recv1[spot].astype(F32)
            if step == 0:
                self.mine[0:SHARE] = part
                if self.extra is not None:
                    self.mine[SHARE] = more
            else:
                self.send2[step - 1, 0:SHARE] = part.astype(BF16)
                if self.extra is not None:
                    self.send2[step - 1, SHARE] = more.astype(BF16)
                copy = remote(
                    self.send2.at[step - 1, pl.ds(0, self.tiles)],
                    self.recv2.at[step - 1, pl.ds(0, self.tiles)],
                    *self.pair(1, step - 1),
                    self.place.in_plane(step),
                )
                self.second.append(self.go(copy))

    def stretch(self, step):
        return pl.ds(ZT * lax.rem(self.place.z + step, EW), ZT)

    def to_line(self):
        for copy in self.second:
            copy.wait_recv()
        part = self.mine[0 : self.tiles]
        for step in range(XY - 1):
            part = part + self.recv2[step, 0 : self.tiles].astype(F32)
        self.mine[0 : self.tiles] = part
        self.send3[...] = self.mine[...].astype(BF16)
        self.third = []
        for step in range(1, EW):
            copy = remote(
                self.send3.at[self.stretch(step)],
                self.recv3.at[step - 1],
                *self.pair(2, step - 1),
                self.place.on_line(step),
            )
            self.third.append(self.go(copy))

    def back_line(self):
        for copy in self.third:
            copy.wait_recv()
        part = self.mine[self.stretch(0)]
        for step in range(EW - 1):
            part = part + self.recv3[step].astype(F32)
        here = self.line.at[self.stretch(0)]
        here[...] = part.astype(BF16)
        self.fourth = []
        for step in range(1, EW):
            copy = remote(here, here, *self.pair(3, step - 1), self.place.on_line(step))
            self.fourth.append(self.go(copy))

    def back_plane(self):
        for copy in self.fourth:
            copy.wait_recv()
        core, chip = self.place.core, self.place.chip
        used = pl.ds(0, self.tiles)
        share, mine = self.line.at[used], self.total.at[core, chip, used]
        self.fifth = []
        for step in range(1, XY):
            copy = remote(share, mine, *self.pair(4, step - 1), self.place.in_plane(step))
            self.fifth.append(self.go(copy))
        self.sixth = [self.go(remote(share, mine, *self.pair(5, 0), self.place.twin()))]
        mine[...] = share[...]

    def back_twin(self):
        for step, copy in enumerate(self.fifth):
            copy.wait_recv()
            came = self.total.at[
                self.place.core,
                lax.rem(self.place.chip + XY - (step + 1), XY),
                pl.ds(0, self.tiles),
            ]
            copy = remote(came, came, *self.pair(5, step + 1), self.place.twin())
            self.sixth.append(self.go(copy))
        for copy in self.sixth:
            copy.wait_recv()

    def close(self):
        for copy in self.started:
            copy.wait_send()


def step_kernel(
    index,
    x_in,
    cot_in,
    mask_in,
    taps_in,
    gain_in,
    shift_in,
    out_bias_in,
    scale_in,
    bias_in,
    win_hbm,
    wout_hbm,
    anchor_in,
    anchor_out,
    totals,
    cycle_came,
    cells_t,
    x_rows,
    cot_rows,
    weights,
    anchors,
    ahead,
    rows_t,
    cols,
    bias_col,
    win_b,
    win_tb,
    wout_tb,
    wout_b,
    shifts,
    spread,
    windows,
    halo,
    conv,
    normed,
    inv_std,
    norm_b,
    hidden,
    slope,
    act_b,
    flow,
    back_b,
    hid_b,
    conv_grad,
    grad_w,
    grad_k,
    out_rows,
    out_edges,
    in_rows,
    in_edges,
    send1,
    recv1,
    own,
    mine,
    send2,
    recv2,
    send3,
    recv3,
    line,
    cycle_out,
    halo_sent,
    halo_came,
    weight_sem,
    anchor_sem,
    cycle_sem,
    *sems,
):
    place = Place()
    barrier = pltpu.get_barrier_semaphore()
    partner = (1 - place.rep, place.z, place.ns)
    peers = [place.twin(), partner]
    peers += [place.in_plane(d) for d in range(1, XY)]
    peers += [place.on_line(d) for d in range(1, EW)]
    peers += [place.beside(dz, dn) for dz, dn in AROUND]
    for peer in peers:
        pl.semaphore_signal(barrier, inc=1, device_id=peer, device_id_type=MESH)
    fetched = [
        pltpu.make_async_copy(anchor_in, anchors.at[0], anchor_sem.at[0]),
        pltpu.make_async_copy(anchor_out, anchors.at[1], anchor_sem.at[1]),
    ]
    loaded = [
        pltpu.make_async_copy(win_hbm, weights.at[0], weight_sem.at[0]),
        pltpu.make_async_copy(wout_hbm, weights.at[1], weight_sem.at[1]),
    ]
    for copy in loaded + fetched:
        copy.start()
    win, wout_t = weights.at[0], weights.at[1]

    def lanes(x):
        return slice(CY * x, CY * (x + 1))

    halos = [
        Halo(
            place,
            turn,
            (x_rows, out_rows.at[0], out_rows.at[1])[turn],
            out_edges,
            in_rows,
            in_edges,
            halo_sent,
            halo_came,
        )
        for turn in range(3)
    ]
    sums = [
        Sum(
            place,
            SHARES[layer],
            send1.at[layer],
            recv1.at[layer],
            own.at[layer],
            mine.at[layer],
            send2.at[layer],
            recv2.at[layer],
            send3.at[layer],
            recv3.at[layer],
            line.at[layer],
            totals.at[layer],
            sems[12 * layer : 12 * (layer + 1)],
        )
        for layer in range(LAYERS)
    ]

    def prepare(layer):
        rows_t[...] = jnp.zeros_like(rows_t)
        rows_t[0:49, 0:C] = taps_in[:, layer, :]
        for row, vector in (
            (GAIN, gain_in),
            (SHIFT, shift_in),
            (OUT_BIAS, out_bias_in),
            (SCALE, scale_in),
        ):
            rows_t[row : row + 1, 0:C] = vector[layer : layer + 1, :]
        cols[layer] = rows_t[...].T[:C]
        win_tb[layer] = win[layer].T.astype(BF16)
        wout_tb[layer] = wout_t[layer].astype(BF16)
        spread_taps(cols.at[layer], spread.at[layer])

    def prepare_back(layer):
        win_b[layer] = win[layer].astype(BF16)
        wout_b[layer] = wout_t[layer].T.astype(BF16)

    ocean = [mask_in[x : x + 1, :].astype(F32) for x in range(CX)]

    def column(layer, which):
        return cols[layer, :, which : which + 1]

    def forward(layer):
        halos[layer].near(shifts, halo, windows.at[layer])
        depthwise(windows.at[layer], spread.at[layer], conv, False, True)
        halos[layer].far(shifts, halo, windows.at[layer])
        depthwise(windows.at[layer], spread.at[layer], conv, False, False)
        for x in range(CX):
            cells = conv[x]
            centered = cells - jnp.mean(cells, axis=0, keepdims=True)
            inv = lax.rsqrt(jnp.mean(centered * centered, axis=0, keepdims=True) + EPSILON)
            unit = centered * inv
            inv_std[layer, x : x + 1, :] = inv
            normed[layer, x] = unit
            norm_b[layer, :, lanes(x)] = (
                unit * column(layer, GAIN) + column(layer, SHIFT)
            ).astype(BF16)
        hidden[...] = dot(win_tb[layer], norm_b[layer])

        @pl.loop(0, HID // 192)
        def _(block):
            at = pl.ds(block * 192, 192)
            pre = hidden[at, :] + bias_col[at, layer : layer + 1]
            bend = (GELU_C * GELU_D) * (pre * pre)
            gate = 0.5 + 0.5 * jnp.tanh(pre * (GELU_C + bend))
            value = pre * gate
            act_b[layer, at, :] = value.astype(BF16)
            slope[layer, at, :] = gate + 2.0 * value * (1.0 - gate) * (GELU_C + 3.0 * bend)

    def output(layer):
        branch = dot(wout_tb[layer], act_b[layer])
        for x in range(CX):
            inner = branch[:, lanes(x)] + column(layer, OUT_BIAS)
            value = ocean[x] * (windows[layer, MAIN + x] + column(layer, SCALE) * inner)
            value = value.astype(BF16)
            out_rows[0, x] = value
            windows[layer + 1, MAIN + x] = value.astype(F32)

    def backward(layer):
        for x in range(CX):
            masked = ocean[x] * flow[x]
            flow[x] = masked
            back_b[:, lanes(x)] = (masked * column(layer, SCALE)).astype(BF16)
        grad_w[layer, 1] = dot_cells(back_b[...], act_b[layer])
        hidden[...] = dot(wout_b[layer], back_b[...])

        @pl.loop(0, HID // 192)
        def _(block):
            at = pl.ds(block * 192, 192)
            hid_b[at, :] = (hidden[at, :] * slope[layer, at, :]).astype(BF16)

        grad_w[layer, 0] = dot_cells(norm_b[layer], hid_b[...])

    def backward_norm(layer):
        norm_grad = dot(win_b[layer], hid_b[...])
        for x in range(CX):
            part = norm_grad[:, lanes(x)] * column(layer, GAIN)
            unit = normed[layer, x]
            mean_grad = jnp.mean(part, axis=0, keepdims=True)
            mean_cross = jnp.mean(part * unit, axis=0, keepdims=True)
            value = inv_std[layer, x : x + 1, :] * (part - mean_grad - unit * mean_cross)
            conv_grad[x] = value
            if layer > 0:
                out_rows[1, x] = value.astype(BF16)

    def by_rows(cells_in, out):
        cells_t[...] = cells_in[...].astype(F32)
        for x in range(CX):
            out[x] = cells_t[pl.ds(x, C, stride=CX), :].astype(BF16)

    def block_at(shape):
        return jnp.full(shape, index[0] // 2, jnp.int32)

    def joined(first, second):
        odd = jnp.full((C, 128), lax.rem(index[0], 2), jnp.int32) == 1
        first = jnp.where(odd, pltpu.roll(first, 64, 1), first)
        second = jnp.where(odd, second, pltpu.roll(second, 64, 1))
        return jnp.where(lanes_of((C, 128)) < 64, first, second)

    def stretch_ahead():
        for copy in fetched:
            copy.wait()
        chosen = [jnp.zeros((C, 128), F32), jnp.zeros((C, 128), F32)]
        for which in range(LAYERS):
            for col in range(6):
                hit = block_at((C, 128)) == 6 * which + col
                for mat, weights in enumerate((win, wout_t)):
                    at = (which, slice(0, C), slice(128 * col, 128 * (col + 1)))
                    chosen[mat] = jnp.where(hit, anchors[(mat,) + at] - weights[at], chosen[mat])
        ahead[...] = joined(*chosen)

    by_rows(x_in, x_rows)
    pl.semaphore_wait(barrier, len(peers))
    halos[0].start()
    for x in range(CX):
        windows[0, MAIN + x] = x_rows[x].astype(F32)
    shifts[...] = shift_matrix()
    bias_rows = jnp.concatenate([bias_in[...], jnp.zeros((128 - LAYERS, HID), F32)], axis=0)
    bias_col[...] = bias_rows.T
    for copy in loaded:
        copy.wait()
    prepare(0)
    forward(0)
    output(0)
    halos[1].start()
    prepare(1)
    stretch_ahead()
    for layer in range(LAYERS):
        prepare_back(layer)
    by_rows(cot_in, cot_rows)
    for x in range(CX):
        flow[x] = cot_rows[x].astype(F32) * (1.0 / 256.0)
    forward(1)
    backward(1)
    backward_norm(1)
    halos[2].start()
    sums[1].start(grad_w.at[1])
    kernel_grad(windows.at[1], conv_grad, grad_k, 64, True)
    sums[1].to_plane()
    for x in range(CX):
        windows[1, MAIN + x] = conv_grad[x]
    halos[2].near(shifts, halo, windows.at[1])
    depthwise(windows.at[1], spread.at[1], conv, True, True)
    halos[2].far(shifts, halo, windows.at[1])
    depthwise(windows.at[1], spread.at[1], conv, True, False)
    for x in range(CX):
        flow[x] = flow[x] + conv[x]
    sums[1].to_line()
    backward(0)
    sums[0].start(grad_w.at[0])
    backward_norm(0)
    sums[1].back_line()
    kernel_grad(windows.at[0], conv_grad, grad_k, 0, False)
    sums[0].start_extra(grad_k)
    sums[0].to_plane()
    sums[0].to_line()
    sums[1].back_plane()
    sums[0].back_line()
    sums[0].back_plane()
    sums[1].back_twin()
    sums[0].back_twin()
    chosen = [jnp.zeros((C, 128), BF16), jnp.zeros((C, 128), BF16)]
    for which in range(LAYERS):
        for col in range(6):
            hit = block_at((C, 128)) == 6 * which + col
            for mat in range(2):
                tiles = [totals[(which, mat) + divmod(6 * row + col, SHARE)] for row in range(12)]
                chosen[mat] = jnp.where(hit, jnp.concatenate(tiles, axis=0), chosen[mat])
    grads = joined(chosen[0].astype(F32), chosen[1].astype(F32))
    cycle_out[...] = (ahead[...] + STEP_RATE * grads).astype(BF16)
    passed = remote(cycle_out, cycle_came, cycle_sem.at[0], cycle_sem.at[1], partner)
    passed.start()
    for each in halos + sums:
        each.close()
    passed.wait()


def whole_step(*operands):
    dma = pltpu.SemaphoreType.DMA
    vmem = pltpu.VMEM
    sums = ([dma((9,))] * 2 + [dma((7,))] * 8 + [dma((8,))] * 2) * LAYERS
    return pl.pallas_call(
        step_kernel,
        out_shape=[
            jax.ShapeDtypeStruct((LAYERS, 2, XY, SHARE + 1, 16, 128), BF16),
            jax.ShapeDtypeStruct((C, 128), BF16),
        ],
        in_specs=[pl.BlockSpec(memory_space=pltpu.SMEM)]
        + [pl.BlockSpec(memory_space=pltpu.VMEM)] * 9
        + [pl.BlockSpec(memory_space=pl.ANY)] * 4,
        out_specs=[pl.BlockSpec(memory_space=pltpu.VMEM)] * 2,
        scratch_shapes=[
            vmem((C * CX, CY), F32),
            vmem((CX, C, CY), BF16),
            vmem((CX, C, CY), BF16),
            vmem((2, LAYERS, C, HID), F32),
            vmem((2, LAYERS, C, HID), F32),
            vmem((C, 128), F32),
            vmem((128, 256), F32),
            vmem((LAYERS, C, 128), F32),
            vmem((HID, 128), F32),
            vmem((LAYERS, C, HID), BF16),
            vmem((LAYERS, HID, C), BF16),
            vmem((LAYERS, C, HID), BF16),
            vmem((LAYERS, HID, C), BF16),
            vmem((2 * CY, 6 * CY), BF16),
            vmem((LAYERS, 49, C, CY), F32),
            vmem((LAYERS, 7 * ROWS, C, CY), F32),
            vmem((ROWS, C, CY), BF16),
            vmem((CX, C, CY), F32),
            vmem((LAYERS, CX, C, CY), F32),
            vmem((LAYERS, CX, CY), F32),
            vmem((LAYERS, C, CELLS), BF16),
            vmem((HID, CELLS), F32),
            vmem((LAYERS, HID, CELLS), F32),
            vmem((LAYERS, HID, CELLS), BF16),
            vmem((CX, C, CY), F32),
            vmem((C, CELLS), BF16),
            vmem((HID, CELLS), BF16),
            vmem((CX, C, CY), F32),
            vmem((LAYERS, 2, C, HID), F32),
            vmem((C, 128), F32),
            vmem((2, CX, C, CY), BF16),
            vmem((3, FOLDED, CY), BF16),
            vmem((3, 2, 3, C, CY), BF16),
            vmem((3, 2, 3, FOLDED, CY), BF16),
            vmem((LAYERS, 80, 16, 128), BF16),
            vmem((LAYERS, 80, 16, 128), BF16),
            vmem((LAYERS, 80, 16, 128), F32),
            vmem((LAYERS, EW * ZT, 16, 128), F32),
            vmem((LAYERS, XY - 1, SHARE + 1, 16, 128), BF16),
            vmem((LAYERS, XY - 1, SHARE + 1, 16, 128), BF16),
            vmem((LAYERS, EW * ZT, 16, 128), BF16),
            vmem((LAYERS, EW - 1, ZT, 16, 128), BF16),
            vmem((LAYERS, EW * ZT, 16, 128), BF16),
            vmem((C, 128), BF16),
            dma((3, 8)),
            dma((3, 8)),
            dma((2,)),
            dma((2,)),
            dma((2,)),
        ]
        + sums,
        compiler_params=pltpu.CompilerParams(
            collective_id=0, has_side_effects=True, vmem_limit_bytes=60 * 2**20
        ),
    )(*operands)


def update_kernel(
    totals, stretch, win, wout_t, taps_in, new_in, new_out, new_k, cycle_in, cycle_out
):
    for layer in range(LAYERS):
        for tile in range(72):
            row, col = divmod(tile, 6)
            at = (layer, slice(16 * row, 16 * (row + 1)), slice(128 * col, 128 * (col + 1)))
            spot = divmod(tile, SHARE)
            new_in[at] = win[at] - STEP_RATE * totals[(layer, 0) + spot].astype(F32)
            new_out[at] = wout_t[at] - STEP_RATE * totals[(layer, 1) + spot].astype(F32)
    grads = [totals[0, half, tile, SHARE].astype(F32) for half in range(2) for tile in range(6)]
    taps = jnp.concatenate(grads, axis=0).T
    for layer in range(LAYERS):
        new_k[:, layer, :] = taps_in[:, layer, :] - STEP_RATE * taps[64 * layer : 64 * layer + 49]
    turned = stretch[...].astype(F32).T
    cycle_in[...] = turned[0:64]
    cycle_out[...] = turned[64:128]


def update(totals, stretch, win, wout_t, taps):
    weights = jax.ShapeDtypeStruct((LAYERS, C, HID), F32)
    part = jax.ShapeDtypeStruct((64, C), F32)
    return pl.pallas_call(
        update_kernel,
        out_shape=[weights, weights, jax.ShapeDtypeStruct((49, LAYERS, C), F32), part, part],
        in_specs=[pl.BlockSpec(memory_space=pltpu.VMEM)] * 5,
        out_specs=[pl.BlockSpec(memory_space=pltpu.VMEM)] * 5,
        compiler_params=pltpu.CompilerParams(vmem_limit_bytes=40 * 2**20),
    )(totals, stretch, win, wout_t, taps)


def body(
    fields,
    cotangent,
    land_mask,
    stretch_index,
    depth_kernel,
    norm_gain,
    norm_bias,
    weight_in,
    bias_in,
    weight_out,
    bias_out,
    layer_scale,
    anchor_in,
    anchor_out,
):
    win = weight_in[0]
    wout_t = weight_out[0].transpose(0, 2, 1)
    taps = depth_kernel[0].transpose(2, 0, 1)
    totals, stretch = whole_step(
        stretch_index,
        fields.reshape(C * CX, CY),
        cotangent.reshape(C * CX, CY),
        land_mask,
        taps,
        norm_gain[0],
        norm_bias[0],
        bias_out[0],
        layer_scale[0],
        bias_in[0],
        win,
        wout_t,
        anchor_in,
        anchor_out.transpose(0, 2, 1),
    )
    new_in, new_out, new_k, cycle_in, cycle_out = update(totals, stretch, win, wout_t, taps)
    return (
        new_k.transpose(1, 2, 0)[None],
        new_in[None],
        new_out.transpose(0, 2, 1)[None],
        cycle_in.T[None],
        cycle_out[None],
    )


def solution(mesh):
    in_specs = (
        P("rep", None, "ew", "ns"),
        P("rep", None, "ew", "ns"),
        P("ew", "ns"),
        P(),
        P("rep", None, None, None),
        P("rep", None, None),
        P("rep", None, None),
        P("rep", None, None, None),
        P("rep", None, None),
        P("rep", None, None, None),
        P("rep", None, None),
        P("rep", None, None),
        P(),
        P(),
    )
    out_specs = (
        P("rep", None, None, None),
        P("rep", None, None, None),
        P("rep", None, None, None),
        P("rep", None, None),
        P("rep", None, None),
    )
    return jax.shard_map(body, mesh=mesh, in_specs=in_specs, out_specs=out_specs, check_vma=False)
```

```python
import jax
import jax.numpy as jnp
from jax import lax
from jax.experimental import pallas as pl
from jax.experimental.pallas import tpu as pltpu
from jax.sharding import PartitionSpec as P

EPSILON = 1e-06
STEP_RATE = 0.1
GELU_C = 0.7978845608028654
GELU_D = 0.044715

MESH = pl.DeviceIdType.MESH
F32 = jnp.float32
BF16 = jnp.bfloat16
C = 192
HID = 768
LAYERS = 2
CX = 4
CY = 128
CELLS = CX * CY
ROWS = CX + 6
BLOCKS = C // 8
FOLD = 4
CUTS = 3
CUT = C // CUTS
FOLDED = C // FOLD
XY = 8
EW = 8
SHIFTED = (0, 1, 2, 4, 5, 6)
NS = 16
ZT = 2
GAIN, SHIFT, OUT_BIAS, SCALE = 49, 50, 51, 52
SHARE = 9
MAIN = 3 * ROWS + 3
SHARES = (10, 9)


def remote(src, dst, send_sem, recv_sem, device):
    return pltpu.make_async_remote_copy(
        src_ref=src,
        dst_ref=dst,
        send_sem=send_sem,
        recv_sem=recv_sem,
        device_id=device,
        device_id_type=MESH,
    )


def lanes_of(shape):
    return lax.broadcasted_iota(jnp.int32, shape, 1)


def dot(left, right):
    return jnp.dot(left, right, preferred_element_type=F32)


def dot_cells(left, right):
    return lax.dot_general(left, right, (((1,), (1,)), ((), ())), preferred_element_type=F32)


class Place:
    def __init__(self):
        self.rep = lax.axis_index("rep")
        self.z = lax.axis_index("ew")
        self.ns = lax.axis_index("ns")
        self.core = lax.rem(self.ns, 2)
        self.chip = self.ns // 2

    def twin(self):
        return (self.rep, self.z, 2 * self.chip + 1 - self.core)

    def in_plane(self, step):
        return (self.rep, self.z, 2 * lax.rem(self.chip + step, XY) + self.core)

    def on_line(self, step):
        return (self.rep, lax.rem(self.z + step, EW), self.ns)

    def beside(self, step_z, step_ns):
        return (
            self.rep,
            lax.rem(self.z + EW + step_z, EW),
            lax.rem(self.ns + NS + step_ns, NS),
        )


AROUND = [(dz, dn) for dn in (1, -1) for dz in (-1, 0, 1)]


class Halo:
    def __init__(self, place, turn, rows, out_edges, in_rows, in_edges, sent, came):
        self.place = place
        self.rows = rows
        self.out_edges = out_edges.at[turn]
        self.in_rows = in_rows.at[turn]
        self.in_edges = in_edges.at[turn]
        self.sent = sent.at[turn]
        self.came = came.at[turn]
        self.row_copies = []
        self.edge_copies = []

    def send_rows(self, cut):
        at = pl.ds(CUT * cut, CUT)
        for number, (first, step) in enumerate(((1, 1), (0, -1))):
            copy = remote(
                self.rows.at[pl.ds(first, 3), at],
                self.in_rows.at[number, :, at],
                self.sent.at[2 * cut + number],
                self.came.at[2 * cut + number],
                self.place.beside(step, 0),
            )
            copy.start()
            self.row_copies.append(copy)

    def start(self):
        place = self.place
        self.send_rows(0)
        slot = ((lanes_of((FOLDED, CY)) + 4) % CY) // 8
        folded = jnp.zeros((FOLDED, CY), F32)
        for x in range(CX):
            row = self.rows[x].astype(F32)
            for part in range(FOLD):
                piece = row[FOLDED * part : FOLDED * (part + 1), :]
                number = 4 * part + x
                moved = pltpu.roll(piece, 8 * number, 1) if number else piece
                folded = jnp.where(slot == number, moved, folded)
        self.out_edges[...] = folded.astype(BF16)
        for number, (dz, dn) in enumerate(AROUND):
            side = 0 if dn == 1 else 1
            copy = remote(
                self.out_edges,
                self.in_edges.at[side, 1 - dz],
                self.sent.at[2 * CUTS + number],
                self.came.at[2 * CUTS + number],
                place.beside(dz, dn),
            )
            copy.start()
            self.edge_copies.append(copy)
        for cut in range(1, CUTS):
            self.send_rows(cut)

    def near(self, shifts, halo, windows):
        for copy in self.edge_copies:
            copy.wait_recv()
        keep_left = (self.place.ns > 0).astype(F32)
        keep_right = (self.place.ns < NS - 1).astype(F32)
        low = (lanes_of((FOLDED, CY)) + 4) % 8 < 4
        for index in range(3):
            edges = jnp.where(
                low,
                self.in_edges[0, index].astype(F32) * keep_left,
                self.in_edges[1, index].astype(F32) * keep_right,
            )
            for x in range(CX):
                row = (x - 1, x + 3, x + 7)[index]
                if (index == 0 and x == 0) or (index == 2 and x == 3):
                    continue
                for part in range(FOLD):
                    number = 4 * part + x
                    moved = pltpu.roll(edges, CY - 8 * number, 1) if number else edges
                    halo[row, FOLDED * part : FOLDED * (part + 1), :] = moved.astype(BF16)

        cells = jnp.concatenate(
            [self.rows[...].reshape(CX * C, CY), halo[3 : 3 + CX].reshape(CX * C, CY)], axis=1
        )
        moved = dot(cells, shifts[...])
        for place, col in enumerate(SHIFTED):
            start = col * ROWS + 3
            part = moved[:, CY * place : CY * (place + 1)]
            windows[start : start + CX] = part.reshape(CX, C, CY)

    def far(self, shifts, halo, windows, cut):
        for copy in self.row_copies[2 * cut : 2 * cut + 2]:
            copy.wait_recv()
        at = slice(CUT * cut, CUT * (cut + 1))
        cells = []
        for side, first in ((0, 0), (1, CX + 3)):
            rows = self.in_rows[side, :, at]
            rims = halo[first : first + 3, at]
            cells.append(
                jnp.concatenate([rows.reshape(3 * CUT, CY), rims.reshape(3 * CUT, CY)], axis=1)
            )
            start = 3 * ROWS + first
            windows[start : start + 3, at] = rows.astype(F32)
        moved = dot(jnp.concatenate(cells, axis=0), shifts[...])
        for side, first in ((0, 0), (1, CX + 3)):
            for place, col in enumerate(SHIFTED):
                start = col * ROWS + first
                part = moved[3 * CUT * side : 3 * CUT * (side + 1), CY * place : CY * (place + 1)]
                windows[start : start + 3, at] = part.reshape(3, CUT, CY)

    def close(self):
        for copy in self.row_copies + self.edge_copies:
            copy.wait_send()


def shift_matrix():
    source = lax.broadcasted_iota(jnp.int32, (2 * CY, CY), 0)
    lane = lanes_of((2 * CY, CY))
    parts = []
    for col in SHIFTED:
        wanted = lane + (col - 3)
        hit = (source == wanted) | (source == wanted + 2 * CY)
        parts.append(hit.astype(F32).astype(BF16))
    return jnp.concatenate(parts, axis=1)


def spread_taps(cols, out):
    parts = []
    for layer in range(LAYERS):
        taps = cols[layer]
        high = taps.astype(BF16).astype(F32)
        middle = (taps - high).astype(BF16).astype(F32)
        parts.append(
            jnp.concatenate([high + pltpu.roll(middle, 64, 1), taps - high - middle], axis=1)
        )
    left = jnp.concatenate(parts, axis=0).astype(BF16)
    source = lax.broadcasted_iota(jnp.int32, (256, 128), 0) % 64
    for tap in range(0, 50, 2):
        picks = [(source == tap + side).astype(F32).astype(BF16) for side in range(2)]
        moved = dot(left, jnp.concatenate(picks, axis=1))
        for layer in range(LAYERS):
            rows = slice(C * layer, C * (layer + 1))
            out[layer, tap] = moved[rows, 0:CY]
            out[layer, tap + 1] = moved[rows, CY : 2 * CY]


def depthwise(windows, spread, out, reverse, own, first=0, blocks=BLOCKS):
    @pl.loop(first, first + blocks, unroll=4)
    def _(block):
        at = pl.ds(block * 8, 8)
        total = [None if own else out[x, at, :] for x in range(CX)]
        used = [row for row in range(ROWS) if (3 <= row < 3 + CX) == own]
        for col in range(7):
            rows = {row: windows[col * ROWS + row, at, :] for row in used}
            part = [None] * CX
            for tap_row in range(7):
                if not any(x + tap_row in rows for x in range(CX)):
                    continue
                tap = 7 * tap_row + col
                weight = spread[48 - tap if reverse else tap, at, :]
                for x in range(CX):
                    if x + tap_row in rows:
                        term = weight * rows[x + tap_row]
                        part[x] = term if part[x] is None else part[x] + term
            for x in range(CX):
                if part[x] is not None:
                    total[x] = part[x] if total[x] is None else total[x] + part[x]
        for x in range(CX):
            out[x, at, :] = total[x]


def kernel_grad(windows, conv_grad, out, lane_base, first):
    @pl.loop(0, BLOCKS, unroll=8)
    def _(block):
        at = pl.ds(block * 8, 8)
        lane = lanes_of((8, CY))
        grads = [conv_grad[x, at, :] for x in range(CX)]
        result = jnp.zeros((8, CY), F32)
        for col in range(7):
            rows = [windows[col * ROWS + row, at, :] for row in range(ROWS)]
            for tap_row in range(7):
                total = grads[0] * rows[tap_row]
                for x in range(1, CX):
                    total = total + grads[x] * rows[x + tap_row]
                tap = 7 * tap_row + col
                result = jnp.where(
                    lane == tap + lane_base, jnp.sum(total, axis=1, keepdims=True), result
                )
        if first:
            out[at, :] = result
        else:
            out[at, :] = out[at, :] + result


class Sum:
    def __init__(
        self, place, tiles, send1, recv1, own, mine, send2, recv2, send3, recv3, line, total, sems
    ):
        self.place = place
        self.tiles = tiles
        self.send1, self.recv1, self.own, self.mine = send1, recv1, own, mine
        self.send2, self.recv2, self.send3, self.recv3 = send2, recv2, send3, recv3
        self.line = line
        self.total = total
        self.sems = sems
        self.started = []
        self.extra = None

    def go(self, copy):
        copy.start()
        self.started.append(copy)
        return copy

    def pair(self, phase, step):
        return self.sems[2 * phase].at[step], self.sems[2 * phase + 1].at[step]

    def pack(self, grads, half, dst):
        @pl.loop(0, 12, unroll=2)
        def _(row):
            for col in range(6):
                dst[row * 6 + col] = grads[
                    half, pl.ds(row * 16, 16), 128 * col : 128 * (col + 1)
                ].astype(dst.dtype)

    def pack_extra(self, extra, half, dst):
        for block in range(6):
            dst[72 + block] = extra[pl.ds(half * 96 + 16 * block, 16), :].astype(dst.dtype)
        dst[78:80] = jnp.zeros((2, 16, 128), dst.dtype)

    def chunk(self, step):
        return lax.rem(self.place.chip + step, XY)

    def share(self, step):
        return pl.ds(SHARE * self.chunk(step), SHARE)

    def start(self, grads):
        core = self.place.core
        self.pack(grads, 1 - core, self.send1)
        self.first = []
        for step in list(range(1, XY)) + [0]:
            part = self.share(step)
            copy = remote(
                self.send1.at[part], self.recv1.at[part], *self.pair(0, step), self.place.twin()
            )
            self.first.append((step, self.go(copy)))
        self.pack(grads, core, self.own)

    def start_extra(self, extra):
        core = self.place.core
        self.pack_extra(extra, 1 - core, self.send1)
        part = pl.ds(72, 8)
        self.extra = self.go(
            remote(self.send1.at[part], self.recv1.at[part], *self.pair(0, 8), self.place.twin())
        )
        self.pack_extra(extra, core, self.own)

    def to_plane(self):
        self.second = []
        self.mine[...] = jnp.zeros_like(self.mine)
        for step, copy in self.first:
            copy.wait_recv()
            part = self.own[self.share(step)] + self.recv1[self.share(step)].astype(F32)
            if step == 0:
                self.mine[0:SHARE] = part
            else:
                self.send2[step - 1, 0:SHARE] = part.astype(BF16)
                copy = remote(
                    self.send2.at[step - 1, pl.ds(0, SHARE)],
                    self.recv2.at[step - 1, pl.ds(0, SHARE)],
                    *self.pair(1, step - 1),
                    self.place.in_plane(step),
                )
                self.second.append(self.go(copy))

    def extra_to_plane(self):
        self.extra.wait_recv()
        for step in list(range(1, XY)) + [0]:
            spot = 72 + self.chunk(step)
            part = self.own[spot] + self.recv1[spot].astype(F32)
            if step == 0:
                self.mine[SHARE] = part
            else:
                self.send2[step - 1, SHARE] = part.astype(BF16)
                copy = remote(
                    self.send2.at[step - 1, pl.ds(SHARE, 1)],
                    self.recv2.at[step - 1, pl.ds(SHARE, 1)],
                    *self.pair(6, step - 1),
                    self.place.in_plane(step),
                )
                self.second.append(self.go(copy))

    def stretch(self, step):
        return pl.ds(ZT * lax.rem(self.place.z + step, EW), ZT)

    def to_line(self):
        for copy in self.second:
            copy.wait_recv()
        part = self.mine[0 : self.tiles]
        for step in range(XY - 1):
            part = part + self.recv2[step, 0 : self.tiles].astype(F32)
        self.mine[0 : self.tiles] = part
        self.send3[...] = self.mine[...].astype(BF16)
        self.third = []
        for step in range(1, EW):
            copy = remote(
                self.send3.at[self.stretch(step)],
                self.recv3.at[step - 1],
                *self.pair(2, step - 1),
                self.place.on_line(step),
            )
            self.third.append(self.go(copy))

    def back_line(self):
        for copy in self.third:
            copy.wait_recv()
        part = self.mine[self.stretch(0)]
        for step in range(EW - 1):
            part = part + self.recv3[step].astype(F32)
        here = self.line.at[self.stretch(0)]
        here[...] = part.astype(BF16)
        self.fourth = []
        for step in range(1, EW):
            copy = remote(here, here, *self.pair(3, step - 1), self.place.on_line(step))
            self.fourth.append(self.go(copy))

    def back_plane(self):
        for copy in self.fourth:
            copy.wait_recv()
        core, chip = self.place.core, self.place.chip
        used = pl.ds(0, self.tiles)
        share, mine = self.line.at[used], self.total.at[core, chip, used]
        self.fifth = []
        for step in range(1, XY):
            copy = remote(share, mine, *self.pair(4, step - 1), self.place.in_plane(step))
            self.fifth.append(self.go(copy))
        self.sixth = [self.go(remote(share, mine, *self.pair(5, 0), self.place.twin()))]
        mine[...] = share[...]

    def back_twin(self):
        self.forward_twin()
        self.end_twin()

    def forward_twin(self):
        for step, copy in enumerate(self.fifth):
            copy.wait_recv()
            came = self.total.at[
                self.place.core,
                lax.rem(self.place.chip + XY - (step + 1), XY),
                pl.ds(0, self.tiles),
            ]
            copy = remote(came, came, *self.pair(5, step + 1), self.place.twin())
            self.sixth.append(self.go(copy))

    def end_twin(self):
        for copy in self.sixth:
            copy.wait_recv()

    def close(self):
        for copy in self.started:
            copy.wait_send()


def step_kernel(
    index,
    x_in,
    cot_in,
    mask_in,
    taps_in,
    gain_in,
    shift_in,
    out_bias_in,
    scale_in,
    bias_in,
    win_hbm,
    wout_hbm,
    anchor_in,
    anchor_out,
    totals,
    cells_t,
    x_rows,
    cot_rows,
    weights,
    anchors,
    ahead,
    rows_t,
    cols,
    bias_col,
    win_b,
    win_tb,
    wout_tb,
    wout_b,
    shifts,
    spread,
    windows,
    halo,
    conv,
    normed,
    inv_std,
    norm_b,
    hidden,
    slope,
    act_b,
    flow,
    back_b,
    hid_b,
    conv_grad,
    grad_w,
    grad_k,
    out_rows,
    out_edges,
    in_rows,
    in_edges,
    send1,
    recv1,
    own,
    mine,
    send2,
    recv2,
    send3,
    recv3,
    line,
    picks,
    came,
    tiles_by,
    ahead_came,
    halo_sent,
    halo_came,
    weight_sem,
    anchor_sem,
    ahead_sem,
    tiles_sem,
    pick_sent,
    pick_came,
    *sems,
):
    place = Place()
    barrier = pltpu.get_barrier_semaphore()
    partner = (1 - place.rep, place.z, place.ns)
    peers = [place.twin()]
    peers += [(1 - place.rep,) + place.in_plane(d)[1:] for d in range(XY)]
    peers += [place.in_plane(d) for d in range(1, XY)]
    peers += [place.on_line(d) for d in range(1, EW)]
    peers += [place.beside(dz, dn) for dz, dn in AROUND]
    for peer in peers:
        pl.semaphore_signal(barrier, inc=1, device_id=peer, device_id_type=MESH)
    fetched = [
        pltpu.make_async_copy(anchor_in, anchors.at[0], anchor_sem.at[0]),
        pltpu.make_async_copy(anchor_out, anchors.at[1], anchor_sem.at[1]),
    ]
    loaded = [
        pltpu.make_async_copy(win_hbm, weights.at[0], weight_sem.at[0]),
        pltpu.make_async_copy(wout_hbm, weights.at[1], weight_sem.at[1]),
    ]
    for copy in loaded + fetched:
        copy.start()
    win, wout_t = weights.at[0], weights.at[1]

    def lanes(x):
        return slice(CY * x, CY * (x + 1))

    halos = [
        Halo(
            place,
            turn,
            (x_rows, out_rows.at[0], out_rows.at[1])[turn],
            out_edges,
            in_rows,
            in_edges,
            halo_sent,
            halo_came,
        )
        for turn in range(3)
    ]
    sums = [
        Sum(
            place,
            SHARES[layer],
            send1.at[layer],
            recv1.at[layer],
            own.at[layer],
            mine.at[layer],
            send2.at[layer],
            recv2.at[layer],
            send3.at[layer],
            recv3.at[layer],
            line.at[layer],
            totals.at[layer],
            sems[14 * layer : 14 * (layer + 1)],
        )
        for layer in range(LAYERS)
    ]

    def columns(layer):
        rows_t[...] = jnp.zeros_like(rows_t)
        rows_t[0:49, 0:C] = taps_in[:, layer, :]
        for row, vector in (
            (GAIN, gain_in),
            (SHIFT, shift_in),
            (OUT_BIAS, out_bias_in),
            (SCALE, scale_in),
        ):
            rows_t[row : row + 1, 0:C] = vector[layer : layer + 1, :]
        cols[layer] = rows_t[...].T[:C]

    def prepare(layer):
        win_tb[layer] = win[layer].T.astype(BF16)
        wout_tb[layer] = wout_t[layer].astype(BF16)

    def prepare_back(layer):
        win_b[layer] = win[layer].astype(BF16)
        wout_b[layer] = wout_t[layer].T.astype(BF16)

    ocean = [mask_in[x : x + 1, :].astype(F32) for x in range(CX)]

    def column(layer, which):
        return cols[layer, :, which : which + 1]

    def outer(turn, layer, reverse):
        for cut in range(CUTS):
            halos[turn].far(shifts, halo, windows.at[layer], cut)
            part = (cut * (CUT // 8), CUT // 8)
            depthwise(windows.at[layer], spread.at[layer], conv, reverse, False, *part)

    def forward(layer):
        halos[layer].near(shifts, halo, windows.at[layer])
        depthwise(windows.at[layer], spread.at[layer], conv, False, True)
        outer(layer, layer, False)
        for x in range(CX):
            cells = conv[x]
            centered = cells - jnp.mean(cells, axis=0, keepdims=True)
            inv = lax.rsqrt(jnp.mean(centered * centered, axis=0, keepdims=True) + EPSILON)
            unit = centered * inv
            inv_std[layer, x : x + 1, :] = inv
            normed[layer, x] = unit
            norm_b[layer, :, lanes(x)] = (
                unit * column(layer, GAIN) + column(layer, SHIFT)
            ).astype(BF16)
        hidden[...] = dot(win_tb[layer], norm_b[layer])

        @pl.loop(0, HID // 192, unroll=4)
        def _(block):
            at = pl.ds(block * 192, 192)
            pre = hidden[at, :] + bias_col[at, layer : layer + 1]
            bend = (GELU_C * GELU_D) * (pre * pre)
            gate = 0.5 + 0.5 * jnp.tanh(pre * (GELU_C + bend))
            value = pre * gate
            act_b[layer, at, :] = value.astype(BF16)
            slope[layer, at, :] = gate + 2.0 * value * (1.0 - gate) * (GELU_C + 3.0 * bend)

    def output(layer):
        branch = dot(wout_tb[layer], act_b[layer])
        for x in range(CX):
            inner = branch[:, lanes(x)] + column(layer, OUT_BIAS)
            value = ocean[x] * (windows[layer, MAIN + x] + column(layer, SCALE) * inner)
            value = value.astype(BF16)
            out_rows[0, x] = value
            windows[layer + 1, MAIN + x] = value.astype(F32)

    def backward(layer):
        for x in range(CX):
            masked = ocean[x] * flow[x]
            flow[x] = masked
            back_b[:, lanes(x)] = (masked * column(layer, SCALE)).astype(BF16)
        grad_w[layer, 1] = dot_cells(back_b[...], act_b[layer])
        hidden[...] = dot(wout_b[layer], back_b[...])

        @pl.loop(0, HID // 192, unroll=4)
        def _(block):
            at = pl.ds(block * 192, 192)
            hid_b[at, :] = (hidden[at, :] * slope[layer, at, :]).astype(BF16)

        grad_w[layer, 0] = dot_cells(norm_b[layer], hid_b[...])

    def backward_norm(layer):
        norm_grad = dot(win_b[layer], hid_b[...])
        for x in range(CX):
            part = norm_grad[:, lanes(x)] * column(layer, GAIN)
            unit = normed[layer, x]
            mean_grad = jnp.mean(part, axis=0, keepdims=True)
            mean_cross = jnp.mean(part * unit, axis=0, keepdims=True)
            value = inv_std[layer, x : x + 1, :] * (part - mean_grad - unit * mean_cross)
            conv_grad[x] = value
            if layer > 0:
                out_rows[1, x] = value.astype(BF16)

    def by_rows(cells_in, out):
        cells_t[...] = cells_in[...].astype(F32)
        for x in range(CX):
            out[x] = cells_t[pl.ds(x, C, stride=CX), :].astype(BF16)

    def hits(shape):
        spot = jnp.full(shape, index[0] // 2, jnp.int32)
        return [
            (layer, col, spot == 6 * layer + col) for layer in range(LAYERS) for col in range(6)
        ]

    def joined(first, second):
        odd = jnp.full((C, 128), lax.rem(index[0], 2), jnp.int32) == 1
        first = jnp.where(odd, pltpu.roll(first, 64, 1), first)
        second = jnp.where(odd, second, pltpu.roll(second, 64, 1))
        return jnp.where(lanes_of((C, 128)) < 64, first, second)

    def stretch_ahead():
        for copy in fetched:
            copy.wait()
        chosen = [jnp.zeros((C, 128), F32), jnp.zeros((C, 128), F32)]
        for layer, col, hit in hits((C, 128)):
            at = (layer, slice(0, C), slice(128 * col, 128 * (col + 1)))
            for mat, weights in enumerate((win, wout_t)):
                chosen[mat] = jnp.where(hit, anchors[(mat,) + at] - weights[at], chosen[mat])
        ahead[...] = joined(*chosen)
        copy = remote(ahead, ahead_came, ahead_sem.at[0], ahead_sem.at[1], partner)
        copy.start()
        return copy

    def stretch_share():
        for slot in range(2):
            picked = jnp.zeros((16, 128), BF16)
            for layer, col, hit in hits((16, 128)):
                at = lax.rem(col + 3 * place.chip, 6) + 6 * slot
                picked = jnp.where(hit, line[layer, at], picked)
            picks[slot] = picked
        copies = []
        for step in range(XY):
            z, ns = place.in_plane(step)[1:]
            copies.append(
                remote(
                    picks, came.at[step], pick_sent.at[step], pick_came.at[step], (1 - place.rep, z, ns)
                )
            )
        for copy in copies:
            copy.start()
        return copies

    def stretch_gather(copies):
        for step, copy in enumerate(copies):
            copy.wait_recv()
            source = lax.rem(place.chip + XY - step, XY)
            tiles_by[place.core, source] = came[step]
        part = tiles_by.at[place.core]
        copy = remote(part, part, tiles_sem.at[0], tiles_sem.at[1], place.twin())
        copy.start()
        return copy

    def stretch_result():
        chosen = [jnp.zeros((C, 128), BF16), jnp.zeros((C, 128), BF16)]
        spot = lax.rem(jnp.full((C, 128), index[0] // 2, jnp.int32), 6)
        for col in range(6):
            for mat in range(2):
                rows = []
                for row in range(12):
                    chip, inside = divmod(6 * row + col, SHARE)
                    rows.append(tiles_by[mat, chip, inside // 6])
                rows = jnp.concatenate(rows, axis=0)
                chosen[mat] = jnp.where(spot == col, rows, chosen[mat])
        grads = joined(chosen[0].astype(F32), chosen[1].astype(F32))
        result = (ahead_came[...] + STEP_RATE * grads).astype(BF16)
        for row in range(12):
            spot = (1,) + divmod(row, XY) + (SHARE,)
            totals[spot] = result[16 * row : 16 * (row + 1), :]
        for row in range(12, 16):
            totals[(1,) + divmod(row, XY) + (SHARE,)] = jnp.zeros((16, 128), BF16)


    by_rows(x_in, x_rows)
    pl.semaphore_wait(barrier, len(peers))
    halos[0].start()
    for x in range(CX):
        windows[0, MAIN + x] = x_rows[x].astype(F32)
    shifts[...] = shift_matrix()
    bias_rows = jnp.concatenate([bias_in[...], jnp.zeros((128 - LAYERS, HID), F32)], axis=0)
    bias_col[...] = bias_rows.T
    for layer in range(LAYERS):
        columns(layer)
    spread_taps(cols, spread)
    for copy in loaded:
        copy.wait()
    prepare(0)
    forward(0)
    output(0)
    halos[1].start()
    prepare(1)
    for layer in range(LAYERS):
        prepare_back(layer)
    by_rows(cot_in, cot_rows)
    for x in range(CX):
        flow[x] = cot_rows[x].astype(F32) * (1.0 / 256.0)
    forward(1)
    backward(1)
    backward_norm(1)
    halos[2].start()
    sums[1].start(grad_w.at[1])
    kernel_grad(windows.at[1], conv_grad, grad_k, 64, True)
    passed = stretch_ahead()
    sums[1].to_plane()
    for x in range(CX):
        windows[1, MAIN + x] = conv_grad[x]
    halos[2].near(shifts, halo, windows.at[1])
    depthwise(windows.at[1], spread.at[1], conv, True, True)
    outer(2, 1, True)
    for x in range(CX):
        flow[x] = flow[x] + conv[x]
    sums[1].to_line()
    backward(0)
    sums[0].start(grad_w.at[0])
    backward_norm(0)
    sums[0].to_plane()
    sums[1].back_line()
    kernel_grad(windows.at[0], conv_grad, grad_k, 0, False)
    sums[0].start_extra(grad_k)
    sums[0].extra_to_plane()
    sums[0].to_line()
    sums[1].back_plane()
    sums[0].back_line()
    sums[0].back_plane()
    picked = stretch_share()
    sums[1].back_twin()
    sums[0].forward_twin()
    joined_copy = stretch_gather(picked)
    sums[0].end_twin()
    passed.wait()
    joined_copy.wait()
    stretch_result()
    for copy in picked:
        copy.wait_send()
    for each in halos + sums:
        each.close()


def whole_step(*operands):
    dma = pltpu.SemaphoreType.DMA
    vmem = pltpu.VMEM
    sums = ([dma((9,))] * 2 + [dma((7,))] * 8 + [dma((8,))] * 2 + [dma((7,))] * 2) * LAYERS
    return pl.pallas_call(
        step_kernel,
        out_shape=jax.ShapeDtypeStruct((LAYERS, 2, XY, SHARE + 1, 16, 128), BF16),
        in_specs=[pl.BlockSpec(memory_space=pltpu.SMEM)]
        + [pl.BlockSpec(memory_space=pltpu.VMEM)] * 9
        + [pl.BlockSpec(memory_space=pl.ANY)] * 4,
        out_specs=pl.BlockSpec(memory_space=pltpu.VMEM),
        scratch_shapes=[
            vmem((C * CX, CY), F32),
            vmem((CX, C, CY), BF16),
            vmem((CX, C, CY), BF16),
            vmem((2, LAYERS, C, HID), F32),
            vmem((2, LAYERS, C, HID), F32),
            vmem((C, 128), F32),
            vmem((128, 256), F32),
            vmem((LAYERS, C, 128), F32),
            vmem((HID, 128), F32),
            vmem((LAYERS, C, HID), BF16),
            vmem((LAYERS, HID, C), BF16),
            vmem((LAYERS, C, HID), BF16),
            vmem((LAYERS, HID, C), BF16),
            vmem((2 * CY, 6 * CY), BF16),
            vmem((LAYERS, 50, C, CY), F32),
            vmem((LAYERS, 7 * ROWS, C, CY), F32),
            vmem((ROWS, C, CY), BF16),
            vmem((CX, C, CY), F32),
            vmem((LAYERS, CX, C, CY), F32),
            vmem((LAYERS, CX, CY), F32),
            vmem((LAYERS, C, CELLS), BF16),
            vmem((HID, CELLS), F32),
            vmem((LAYERS, HID, CELLS), F32),
            vmem((LAYERS, HID, CELLS), BF16),
            vmem((CX, C, CY), F32),
            vmem((C, CELLS), BF16),
            vmem((HID, CELLS), BF16),
            vmem((CX, C, CY), F32),
            vmem((LAYERS, 2, C, HID), F32),
            vmem((C, 128), F32),
            vmem((2, CX, C, CY), BF16),
            vmem((3, FOLDED, CY), BF16),
            vmem((3, 2, 3, C, CY), BF16),
            vmem((3, 2, 3, FOLDED, CY), BF16),
            vmem((LAYERS, 80, 16, 128), BF16),
            vmem((LAYERS, 80, 16, 128), BF16),
            vmem((LAYERS, 80, 16, 128), F32),
            vmem((LAYERS, EW * ZT, 16, 128), F32),
            vmem((LAYERS, XY - 1, SHARE + 1, 16, 128), BF16),
            vmem((LAYERS, XY - 1, SHARE + 1, 16, 128), BF16),
            vmem((LAYERS, EW * ZT, 16, 128), BF16),
            vmem((LAYERS, EW - 1, ZT, 16, 128), BF16),
            vmem((LAYERS, EW * ZT, 16, 128), BF16),
            vmem((2, 16, 128), BF16),
            vmem((XY, 2, 16, 128), BF16),
            vmem((2, XY, 2, 16, 128), BF16),
            vmem((C, 128), F32),
            dma((3, 2 * CUTS + 6)),
            dma((3, 2 * CUTS + 6)),
            dma((2,)),
            dma((2,)),
            dma((2,)),
            dma((2,)),
            dma((8,)),
            dma((8,)),
        ]
        + sums,
        compiler_params=pltpu.CompilerParams(
            collective_id=0, has_side_effects=True, vmem_limit_bytes=60 * 2**20
        ),
    )(*operands)


def update_kernel(
    totals, win, wout_t, taps_in, new_in, new_out, new_k, cycle_in, cycle_out
):
    for layer in range(LAYERS):
        for tile in range(72):
            row, col = divmod(tile, 6)
            at = (layer, slice(16 * row, 16 * (row + 1)), slice(128 * col, 128 * (col + 1)))
            spot = divmod(tile, SHARE)
            new_in[at] = win[at] - STEP_RATE * totals[(layer, 0) + spot].astype(F32)
            new_out[at] = wout_t[at] - STEP_RATE * totals[(layer, 1) + spot].astype(F32)
    grads = [totals[0, half, tile, SHARE].astype(F32) for half in range(2) for tile in range(6)]
    taps = jnp.concatenate(grads, axis=0).T
    for layer in range(LAYERS):
        new_k[:, layer, :] = taps_in[:, layer, :] - STEP_RATE * taps[64 * layer : 64 * layer + 49]
    rows = [totals[(1,) + divmod(row, XY) + (SHARE,)].astype(F32) for row in range(12)]
    turned = jnp.concatenate(rows, axis=0).T
    cycle_in[...] = turned[0:64]
    cycle_out[...] = turned[64:128]


def update(totals, win, wout_t, taps):
    weights = jax.ShapeDtypeStruct((LAYERS, C, HID), F32)
    part = jax.ShapeDtypeStruct((64, C), F32)
    return pl.pallas_call(
        update_kernel,
        out_shape=[weights, weights, jax.ShapeDtypeStruct((49, LAYERS, C), F32), part, part],
        in_specs=[pl.BlockSpec(memory_space=pltpu.VMEM)] * 4,
        out_specs=[pl.BlockSpec(memory_space=pltpu.VMEM)] * 5,
        compiler_params=pltpu.CompilerParams(vmem_limit_bytes=40 * 2**20),
    )(totals, win, wout_t, taps)


def body(
    fields,
    cotangent,
    land_mask,
    stretch_index,
    depth_kernel,
    norm_gain,
    norm_bias,
    weight_in,
    bias_in,
    weight_out,
    bias_out,
    layer_scale,
    anchor_in,
    anchor_out,
):
    win = weight_in[0]
    wout_t = weight_out[0].transpose(0, 2, 1)
    taps = depth_kernel[0].transpose(2, 0, 1)
    totals = whole_step(
        stretch_index,
        fields.reshape(C * CX, CY),
        cotangent.reshape(C * CX, CY),
        land_mask,
        taps,
        norm_gain[0],
        norm_bias[0],
        bias_out[0],
        layer_scale[0],
        bias_in[0],
        win,
        wout_t,
        anchor_in,
        anchor_out.transpose(0, 2, 1),
    )
    new_in, new_out, new_k, cycle_in, cycle_out = update(totals, win, wout_t, taps)
    return (
        new_k.transpose(1, 2, 0)[None],
        new_in[None],
        new_out.transpose(0, 2, 1)[None],
        cycle_in.T[None],
        cycle_out[None],
    )


def solution(mesh):
    in_specs = (
        P("rep", None, "ew", "ns"),
        P("rep", None, "ew", "ns"),
        P("ew", "ns"),
        P(),
        P("rep", None, None, None),
        P("rep", None, None),
        P("rep", None, None),
        P("rep", None, None, None),
        P("rep", None, None),
        P("rep", None, None, None),
        P("rep", None, None),
        P("rep", None, None),
        P(),
        P(),
    )
    out_specs = (
        P("rep", None, None, None),
        P("rep", None, None, None),
        P("rep", None, None, None),
        P("rep", None, None),
        P("rep", None, None),
    )
    return jax.shard_map(body, mesh=mesh, in_specs=in_specs, out_specs=out_specs, check_vma=False)
```

```python
import jax
import jax.numpy as jnp
from jax import lax
from jax.experimental import pallas as pl
from jax.experimental.pallas import tpu as pltpu
from jax.sharding import PartitionSpec as P

EPSILON = 1e-06
STEP_RATE = 0.1
GELU_C = 0.7978845608028654
GELU_D = 0.044715

MESH = pl.DeviceIdType.MESH
F32 = jnp.float32
BF16 = jnp.bfloat16
C = 192
HID = 768
LAYERS = 2
CX = 4
CY = 128
CELLS = CX * CY
ROWS = CX + 6
BLOCKS = C // 8
FOLD = 4
CUTS = 6
CUT = C // CUTS
FOLDED = C // FOLD
XY = 8
EW = 8
SHIFTED = (0, 1, 2, 4, 5, 6)
NS = 16
ZT = 2
GAIN, SHIFT, OUT_BIAS, SCALE = 49, 50, 51, 52
SHARE = 9
MAIN = 3 * ROWS + 3
SHARES = (10, 9)


def remote(src, dst, send_sem, recv_sem, device):
    return pltpu.make_async_remote_copy(
        src_ref=src,
        dst_ref=dst,
        send_sem=send_sem,
        recv_sem=recv_sem,
        device_id=device,
        device_id_type=MESH,
    )


def lanes_of(shape):
    return lax.broadcasted_iota(jnp.int32, shape, 1)


def dot(left, right):
    return jnp.dot(left, right, preferred_element_type=F32)


def dot_cells(left, right):
    return lax.dot_general(left, right, (((1,), (1,)), ((), ())), preferred_element_type=F32)


class Place:
    def __init__(self):
        self.rep = lax.axis_index("rep")
        self.z = lax.axis_index("ew")
        self.ns = lax.axis_index("ns")
        self.core = lax.rem(self.ns, 2)
        self.chip = self.ns // 2

    def twin(self):
        return (self.rep, self.z, 2 * self.chip + 1 - self.core)

    def in_plane(self, step):
        return (self.rep, self.z, 2 * lax.rem(self.chip + step, XY) + self.core)

    def on_line(self, step):
        return (self.rep, lax.rem(self.z + step, EW), self.ns)

    def beside(self, step_z, step_ns):
        return (
            self.rep,
            lax.rem(self.z + EW + step_z, EW),
            lax.rem(self.ns + NS + step_ns, NS),
        )


AROUND = [(dz, dn) for dn in (1, -1) for dz in (-1, 0, 1)]


class Halo:
    def __init__(self, place, turn, rows, out_edges, in_rows, in_edges, sent, came):
        self.place = place
        self.rows = rows
        self.out_edges = out_edges.at[turn]
        self.in_rows = in_rows.at[turn]
        self.in_edges = in_edges.at[turn]
        self.sent = sent.at[turn]
        self.came = came.at[turn]
        self.row_copies = []
        self.edge_copies = []

    def send_rows(self, cut):
        at = pl.ds(CUT * cut, CUT)
        for number, (first, step) in enumerate(((1, 1), (0, -1))):
            copy = remote(
                self.rows.at[pl.ds(first, 3), at],
                self.in_rows.at[number, :, at],
                self.sent.at[2 * cut + number],
                self.came.at[2 * cut + number],
                self.place.beside(step, 0),
            )
            copy.start()
            self.row_copies.append(copy)

    def start(self):
        place = self.place
        slot = ((lanes_of((FOLDED, CY)) + 4) % CY) // 8
        folded = jnp.zeros((FOLDED, CY), F32)
        for x in range(CX):
            row = self.rows[x].astype(F32)
            for part in range(FOLD):
                piece = row[FOLDED * part : FOLDED * (part + 1), :]
                number = 4 * part + x
                moved = pltpu.roll(piece, 8 * number, 1) if number else piece
                folded = jnp.where(slot == number, moved, folded)
        self.out_edges[...] = folded.astype(BF16)
        for number, (dz, dn) in enumerate(AROUND):
            side = 0 if dn == 1 else 1
            copy = remote(
                self.out_edges,
                self.in_edges.at[side, 1 - dz],
                self.sent.at[2 * CUTS + number],
                self.came.at[2 * CUTS + number],
                place.beside(dz, dn),
            )
            copy.start()
            self.edge_copies.append(copy)
        for cut in range(CUTS):
            self.send_rows(cut)

    def near(self, shifts, halo, windows):
        self.rims(halo, (1,))
        cells = jnp.concatenate(
            [self.rows[...].reshape(CX * C, CY), halo[3 : 3 + CX].reshape(CX * C, CY)], axis=1
        )
        moved = dot(cells, shifts[...])
        for place, col in enumerate(SHIFTED):
            start = col * ROWS + 3
            part = moved[:, CY * place : CY * (place + 1)]
            windows[start : start + CX] = part.reshape(CX, C, CY)

    def rims(self, halo, indices):
        for copy, (dz, _) in zip(self.edge_copies, AROUND):
            if 1 - dz in indices:
                copy.wait_recv()
        keep_left = (self.place.ns > 0).astype(F32)
        keep_right = (self.place.ns < NS - 1).astype(F32)
        low = (lanes_of((FOLDED, CY)) + 4) % 8 < 4
        for index in indices:
            edges = jnp.where(
                low,
                self.in_edges[0, index].astype(F32) * keep_left,
                self.in_edges[1, index].astype(F32) * keep_right,
            )
            for x in range(CX):
                row = (x - 1, x + 3, x + 7)[index]
                if (index == 0 and x == 0) or (index == 2 and x == 3):
                    continue
                for part in range(FOLD):
                    number = 4 * part + x
                    moved = pltpu.roll(edges, CY - 8 * number, 1) if number else edges
                    halo[row, FOLDED * part : FOLDED * (part + 1), :] = moved.astype(BF16)

    def far(self, shifts, halo, windows, cut):
        for copy in self.row_copies[2 * cut : 2 * cut + 2]:
            copy.wait_recv()
        at = slice(CUT * cut, CUT * (cut + 1))
        cells = []
        for side, first in ((0, 0), (1, CX + 3)):
            rows = self.in_rows[side, :, at]
            rims = halo[first : first + 3, at]
            cells.append(
                jnp.concatenate([rows.reshape(3 * CUT, CY), rims.reshape(3 * CUT, CY)], axis=1)
            )
            start = 3 * ROWS + first
            windows[start : start + 3, at] = rows.astype(F32)
        moved = dot(jnp.concatenate(cells, axis=0), shifts[...])
        for side, first in ((0, 0), (1, CX + 3)):
            for place, col in enumerate(SHIFTED):
                start = col * ROWS + first
                part = moved[3 * CUT * side : 3 * CUT * (side + 1), CY * place : CY * (place + 1)]
                windows[start : start + 3, at] = part.reshape(3, CUT, CY)

    def close(self):
        for copy in self.row_copies + self.edge_copies:
            copy.wait_send()


def shift_matrix():
    source = lax.broadcasted_iota(jnp.int32, (2 * CY, CY), 0)
    lane = lanes_of((2 * CY, CY))
    parts = []
    for col in SHIFTED:
        wanted = lane + (col - 3)
        hit = (source == wanted) | (source == wanted + 2 * CY)
        parts.append(hit.astype(F32).astype(BF16))
    return jnp.concatenate(parts, axis=1)


def spread_taps(cols, out):
    parts = []
    for layer in range(LAYERS):
        taps = cols[layer]
        high = taps.astype(BF16).astype(F32)
        middle = (taps - high).astype(BF16).astype(F32)
        parts.append(
            jnp.concatenate([high + pltpu.roll(middle, 64, 1), taps - high - middle], axis=1)
        )
    left = jnp.concatenate(parts, axis=0).astype(BF16)
    source = lax.broadcasted_iota(jnp.int32, (256, 128), 0) % 64
    for tap in range(0, 50, 2):
        picks = [(source == tap + side).astype(F32).astype(BF16) for side in range(2)]
        moved = dot(left, jnp.concatenate(picks, axis=1))
        for layer in range(LAYERS):
            rows = slice(C * layer, C * (layer + 1))
            out[layer, tap] = moved[rows, 0:CY]
            out[layer, tap + 1] = moved[rows, CY : 2 * CY]


def depthwise(windows, spread, out, reverse, own, first=0, blocks=BLOCKS):
    @pl.loop(first, first + blocks, unroll=4)
    def _(block):
        at = pl.ds(block * 8, 8)
        total = [None if own else out[x, at, :] for x in range(CX)]
        used = [row for row in range(ROWS) if (3 <= row < 3 + CX) == own]
        for col in range(7):
            rows = {row: windows[col * ROWS + row, at, :] for row in used}
            part = [None] * CX
            for tap_row in range(7):
                if not any(x + tap_row in rows for x in range(CX)):
                    continue
                tap = 7 * tap_row + col
                weight = spread[48 - tap if reverse else tap, at, :]
                for x in range(CX):
                    if x + tap_row in rows:
                        term = weight * rows[x + tap_row]
                        part[x] = term if part[x] is None else part[x] + term
            for x in range(CX):
                if part[x] is not None:
                    total[x] = part[x] if total[x] is None else total[x] + part[x]
        for x in range(CX):
            out[x, at, :] = total[x]


def kernel_grad(windows, conv_grad, out, lane_base, first):
    @pl.loop(0, BLOCKS, unroll=8)
    def _(block):
        at = pl.ds(block * 8, 8)
        lane = lanes_of((8, CY))
        grads = [conv_grad[x, at, :] for x in range(CX)]
        result = jnp.zeros((8, CY), F32)
        for col in range(7):
            rows = [windows[col * ROWS + row, at, :] for row in range(ROWS)]
            for tap_row in range(7):
                total = grads[0] * rows[tap_row]
                for x in range(1, CX):
                    total = total + grads[x] * rows[x + tap_row]
                tap = 7 * tap_row + col
                result = jnp.where(
                    lane == tap + lane_base, jnp.sum(total, axis=1, keepdims=True), result
                )
        if first:
            out[at, :] = result
        else:
            out[at, :] = out[at, :] + result


class Sum:
    def __init__(
        self, place, tiles, send1, recv1, own, mine, send2, recv2, send3, recv3, line, total, sems
    ):
        self.place = place
        self.tiles = tiles
        self.send1, self.recv1, self.own, self.mine = send1, recv1, own, mine
        self.send2, self.recv2, self.send3, self.recv3 = send2, recv2, send3, recv3
        self.line = line
        self.total = total
        self.sems = sems
        self.started = []
        self.extra = None

    def go(self, copy):
        copy.start()
        self.started.append(copy)
        return copy

    def pair(self, phase, step):
        return self.sems[2 * phase].at[step], self.sems[2 * phase + 1].at[step]

    def pack(self, grads, half, dst):
        @pl.loop(0, 12, unroll=2)
        def _(row):
            for col in range(6):
                dst[row * 6 + col] = grads[
                    half, pl.ds(row * 16, 16), 128 * col : 128 * (col + 1)
                ].astype(dst.dtype)

    def pack_extra(self, extra, half, dst):
        for block in range(6):
            dst[72 + block] = extra[pl.ds(half * 96 + 16 * block, 16), :].astype(dst.dtype)
        dst[78:80] = jnp.zeros((2, 16, 128), dst.dtype)

    def chunk(self, step):
        return lax.rem(self.place.chip + step, XY)

    def share(self, step):
        return pl.ds(SHARE * self.chunk(step), SHARE)

    def start(self, grads):
        core = self.place.core
        self.pack(grads, 1 - core, self.send1)
        self.first = []
        for step in list(range(1, XY)) + [0]:
            part = self.share(step)
            copy = remote(
                self.send1.at[part], self.recv1.at[part], *self.pair(0, step), self.place.twin()
            )
            self.first.append((step, self.go(copy)))
        self.pack(grads, core, self.own)

    def start_extra(self, extra):
        core = self.place.core
        self.pack_extra(extra, 1 - core, self.send1)
        part = pl.ds(72, 8)
        self.extra = self.go(
            remote(self.send1.at[part], self.recv1.at[part], *self.pair(0, 8), self.place.twin())
        )
        self.pack_extra(extra, core, self.own)

    def to_plane(self):
        self.second = []
        self.mine[...] = jnp.zeros_like(self.mine)
        for step, copy in self.first:
            copy.wait_recv()
            part = self.own[self.share(step)] + self.recv1[self.share(step)].astype(F32)
            if step == 0:
                self.mine[0:SHARE] = part
            else:
                self.send2[step - 1, 0:SHARE] = part.astype(BF16)
                copy = remote(
                    self.send2.at[step - 1, pl.ds(0, SHARE)],
                    self.recv2.at[step - 1, pl.ds(0, SHARE)],
                    *self.pair(1, step - 1),
                    self.place.in_plane(step),
                )
                self.second.append(self.go(copy))

    def extra_to_plane(self):
        self.extra.wait_recv()
        for step in list(range(1, XY)) + [0]:
            spot = 72 + self.chunk(step)
            part = self.own[spot] + self.recv1[spot].astype(F32)
            if step == 0:
                self.mine[SHARE] = part
            else:
                self.send2[step - 1, SHARE] = part.astype(BF16)
                copy = remote(
                    self.send2.at[step - 1, pl.ds(SHARE, 1)],
                    self.recv2.at[step - 1, pl.ds(SHARE, 1)],
                    *self.pair(6, step - 1),
                    self.place.in_plane(step),
                )
                self.second.append(self.go(copy))

    def stretch(self, step):
        return pl.ds(ZT * lax.rem(self.place.z + step, EW), ZT)

    def to_line(self):
        for copy in self.second:
            copy.wait_recv()
        part = self.mine[0 : self.tiles]
        for step in range(XY - 1):
            part = part + self.recv2[step, 0 : self.tiles].astype(F32)
        self.mine[0 : self.tiles] = part
        self.send3[...] = self.mine[...].astype(BF16)
        self.third = []
        for step in range(1, EW):
            copy = remote(
                self.send3.at[self.stretch(step)],
                self.recv3.at[step - 1],
                *self.pair(2, step - 1),
                self.place.on_line(step),
            )
            self.third.append(self.go(copy))

    def back_line(self):
        for copy in self.third:
            copy.wait_recv()
        part = self.mine[self.stretch(0)]
        for step in range(EW - 1):
            part = part + self.recv3[step].astype(F32)
        here = self.line.at[self.stretch(0)]
        here[...] = part.astype(BF16)
        self.fourth = []
        for step in range(1, EW):
            copy = remote(here, here, *self.pair(3, step - 1), self.place.on_line(step))
            self.fourth.append(self.go(copy))

    def back_plane(self):
        for copy in self.fourth:
            copy.wait_recv()
        core, chip = self.place.core, self.place.chip
        used = pl.ds(0, self.tiles)
        share, mine = self.line.at[used], self.total.at[core, chip, used]
        self.fifth = []
        for step in range(1, XY):
            copy = remote(share, mine, *self.pair(4, step - 1), self.place.in_plane(step))
            self.fifth.append(self.go(copy))
        self.sixth = [self.go(remote(share, mine, *self.pair(5, 0), self.place.twin()))]
        mine[...] = share[...]

    def back_twin(self):
        self.forward_twin()
        self.end_twin()

    def forward_twin(self):
        for step, copy in enumerate(self.fifth):
            copy.wait_recv()
            came = self.total.at[
                self.place.core,
                lax.rem(self.place.chip + XY - (step + 1), XY),
                pl.ds(0, self.tiles),
            ]
            copy = remote(came, came, *self.pair(5, step + 1), self.place.twin())
            self.sixth.append(self.go(copy))

    def end_twin(self):
        for copy in self.sixth:
            copy.wait_recv()

    def close(self):
        for copy in self.started:
            copy.wait_send()


def step_kernel(
    index,
    x_in,
    cot_in,
    mask_in,
    taps_in,
    gain_in,
    shift_in,
    out_bias_in,
    scale_in,
    bias_in,
    win_hbm,
    wout_hbm,
    anchor_in,
    anchor_out,
    totals,
    cells_t,
    x_rows,
    cot_rows,
    weights,
    anchors,
    ahead,
    rows_t,
    cols,
    bias_col,
    win_b,
    win_tb,
    wout_tb,
    wout_b,
    shifts,
    spread,
    windows,
    halo,
    conv,
    normed,
    inv_std,
    norm_b,
    hidden,
    slope,
    act_b,
    flow,
    back_b,
    hid_b,
    conv_grad,
    grad_w,
    grad_k,
    out_rows,
    out_edges,
    in_rows,
    in_edges,
    send1,
    recv1,
    own,
    mine,
    send2,
    recv2,
    send3,
    recv3,
    line,
    picks,
    came,
    tiles_by,
    ahead_came,
    halo_sent,
    halo_came,
    weight_sem,
    anchor_sem,
    ahead_sem,
    tiles_sem,
    pick_sent,
    pick_came,
    *sems,
):
    place = Place()
    barrier = pltpu.get_barrier_semaphore()
    partner = (1 - place.rep, place.z, place.ns)
    peers = [place.twin()]
    peers += [(1 - place.rep,) + place.in_plane(d)[1:] for d in range(XY)]
    peers += [place.in_plane(d) for d in range(1, XY)]
    peers += [place.on_line(d) for d in range(1, EW)]
    peers += [place.beside(dz, dn) for dz, dn in AROUND]
    for peer in peers:
        pl.semaphore_signal(barrier, inc=1, device_id=peer, device_id_type=MESH)
    fetched = [
        pltpu.make_async_copy(anchor_in, anchors.at[0], anchor_sem.at[0]),
        pltpu.make_async_copy(anchor_out, anchors.at[1], anchor_sem.at[1]),
    ]
    loaded = [
        pltpu.make_async_copy(win_hbm, weights.at[0], weight_sem.at[0]),
        pltpu.make_async_copy(wout_hbm, weights.at[1], weight_sem.at[1]),
    ]
    for copy in loaded + fetched:
        copy.start()
    win, wout_t = weights.at[0], weights.at[1]

    def lanes(x):
        return slice(CY * x, CY * (x + 1))

    halos = [
        Halo(
            place,
            turn,
            (x_rows, out_rows.at[0], out_rows.at[1])[turn],
            out_edges,
            in_rows,
            in_edges,
            halo_sent,
            halo_came,
        )
        for turn in range(3)
    ]
    sums = [
        Sum(
            place,
            SHARES[layer],
            send1.at[layer],
            recv1.at[layer],
            own.at[layer],
            mine.at[layer],
            send2.at[layer],
            recv2.at[layer],
            send3.at[layer],
            recv3.at[layer],
            line.at[layer],
            totals.at[layer],
            sems[14 * layer : 14 * (layer + 1)],
        )
        for layer in range(LAYERS)
    ]

    def columns(layer):
        rows_t[...] = jnp.zeros_like(rows_t)
        rows_t[0:49, 0:C] = taps_in[:, layer, :]
        for row, vector in (
            (GAIN, gain_in),
            (SHIFT, shift_in),
            (OUT_BIAS, out_bias_in),
            (SCALE, scale_in),
        ):
            rows_t[row : row + 1, 0:C] = vector[layer : layer + 1, :]
        cols[layer] = rows_t[...].T[:C]

    def prepare(layer):
        win_tb[layer] = win[layer].T.astype(BF16)
        wout_tb[layer] = wout_t[layer].astype(BF16)

    def prepare_back(layer):
        win_b[layer] = win[layer].astype(BF16)
        wout_b[layer] = wout_t[layer].T.astype(BF16)

    ocean = [mask_in[x : x + 1, :].astype(F32) for x in range(CX)]

    def column(layer, which):
        return cols[layer, :, which : which + 1]

    def outer(turn, layer, reverse):
        halos[turn].rims(halo, (0, 2))
        for cut in range(CUTS):
            halos[turn].far(shifts, halo, windows.at[layer], cut)
            part = (cut * (CUT // 8), CUT // 8)
            depthwise(windows.at[layer], spread.at[layer], conv, reverse, False, *part)

    def forward(layer):
        halos[layer].near(shifts, halo, windows.at[layer])
        depthwise(windows.at[layer], spread.at[layer], conv, False, True)
        outer(layer, layer, False)
        for x in range(CX):
            cells = conv[x]
            centered = cells - jnp.mean(cells, axis=0, keepdims=True)
            inv = lax.rsqrt(jnp.mean(centered * centered, axis=0, keepdims=True) + EPSILON)
            unit = centered * inv
            inv_std[layer, x : x + 1, :] = inv
            normed[layer, x] = unit
            norm_b[layer, :, lanes(x)] = (
                unit * column(layer, GAIN) + column(layer, SHIFT)
            ).astype(BF16)
        hidden[...] = dot(win_tb[layer], norm_b[layer])

        @pl.loop(0, HID // 192, unroll=4)
        def _(block):
            at = pl.ds(block * 192, 192)
            pre = hidden[at, :] + bias_col[at, layer : layer + 1]
            bend = (GELU_C * GELU_D) * (pre * pre)
            gate = 0.5 + 0.5 * jnp.tanh(pre * (GELU_C + bend))
            value = pre * gate
            act_b[layer, at, :] = value.astype(BF16)
            slope[layer, at, :] = gate + 2.0 * value * (1.0 - gate) * (GELU_C + 3.0 * bend)

    def output(layer):
        branch = dot(wout_tb[layer], act_b[layer])
        for x in range(CX):
            inner = branch[:, lanes(x)] + column(layer, OUT_BIAS)
            value = ocean[x] * (windows[layer, MAIN + x] + column(layer, SCALE) * inner)
            value = value.astype(BF16)
            out_rows[0, x] = value
            windows[layer + 1, MAIN + x] = value.astype(F32)

    def backward(layer):
        for x in range(CX):
            masked = ocean[x] * flow[x]
            flow[x] = masked
            back_b[:, lanes(x)] = (masked * column(layer, SCALE)).astype(BF16)
        grad_w[layer, 1] = dot_cells(back_b[...], act_b[layer])
        hidden[...] = dot(wout_b[layer], back_b[...])

        @pl.loop(0, HID // 192, unroll=4)
        def _(block):
            at = pl.ds(block * 192, 192)
            hid_b[at, :] = (hidden[at, :] * slope[layer, at, :]).astype(BF16)

        grad_w[layer, 0] = dot_cells(norm_b[layer], hid_b[...])

    def backward_norm(layer):
        norm_grad = dot(win_b[layer], hid_b[...])
        for x in range(CX):
            part = norm_grad[:, lanes(x)] * column(layer, GAIN)
            unit = normed[layer, x]
            mean_grad = jnp.mean(part, axis=0, keepdims=True)
            mean_cross = jnp.mean(part * unit, axis=0, keepdims=True)
            value = inv_std[layer, x : x + 1, :] * (part - mean_grad - unit * mean_cross)
            conv_grad[x] = value
            if layer > 0:
                out_rows[1, x] = value.astype(BF16)

    def by_rows(cells_in, out):
        cells_t[...] = cells_in[...].astype(F32)
        for x in range(CX):
            out[x] = cells_t[pl.ds(x, C, stride=CX), :].astype(BF16)

    def hits(shape):
        spot = jnp.full(shape, index[0] // 2, jnp.int32)
        return [
            (layer, col, spot == 6 * layer + col) for layer in range(LAYERS) for col in range(6)
        ]

    def joined(first, second):
        odd = jnp.full((C, 128), lax.rem(index[0], 2), jnp.int32) == 1
        first = jnp.where(odd, pltpu.roll(first, 64, 1), first)
        second = jnp.where(odd, second, pltpu.roll(second, 64, 1))
        return jnp.where(lanes_of((C, 128)) < 64, first, second)

    def stretch_ahead():
        for copy in fetched:
            copy.wait()
        chosen = [jnp.zeros((C, 128), F32), jnp.zeros((C, 128), F32)]
        for layer, col, hit in hits((C, 128)):
            at = (layer, slice(0, C), slice(128 * col, 128 * (col + 1)))
            for mat, weights in enumerate((win, wout_t)):
                chosen[mat] = jnp.where(hit, anchors[(mat,) + at] - weights[at], chosen[mat])
        ahead[...] = joined(*chosen)
        copy = remote(ahead, ahead_came, ahead_sem.at[0], ahead_sem.at[1], partner)
        copy.start()
        return copy

    def stretch_share():
        for slot in range(2):
            picked = jnp.zeros((16, 128), BF16)
            for layer, col, hit in hits((16, 128)):
                at = lax.rem(col + 3 * place.chip, 6) + 6 * slot
                picked = jnp.where(hit, line[layer, at], picked)
            picks[slot] = picked
        copies = []
        for step in range(XY):
            z, ns = place.in_plane(step)[1:]
            copies.append(
                remote(
                    picks, came.at[step], pick_sent.at[step], pick_came.at[step], (1 - place.rep, z, ns)
                )
            )
        for copy in copies:
            copy.start()
        return copies

    def stretch_gather(copies):
        for step, copy in enumerate(copies):
            copy.wait_recv()
            source = lax.rem(place.chip + XY - step, XY)
            tiles_by[place.core, source] = came[step]
        part = tiles_by.at[place.core]
        copy = remote(part, part, tiles_sem.at[0], tiles_sem.at[1], place.twin())
        copy.start()
        return copy

    def stretch_result():
        chosen = [jnp.zeros((C, 128), BF16), jnp.zeros((C, 128), BF16)]
        spot = lax.rem(jnp.full((C, 128), index[0] // 2, jnp.int32), 6)
        for col in range(6):
            for mat in range(2):
                rows = []
                for row in range(12):
                    chip, inside = divmod(6 * row + col, SHARE)
                    rows.append(tiles_by[mat, chip, inside // 6])
                rows = jnp.concatenate(rows, axis=0)
                chosen[mat] = jnp.where(spot == col, rows, chosen[mat])
        grads = joined(chosen[0].astype(F32), chosen[1].astype(F32))
        result = (ahead_came[...] + STEP_RATE * grads).astype(BF16)
        for row in range(12):
            spot = (1,) + divmod(row, XY) + (SHARE,)
            totals[spot] = result[16 * row : 16 * (row + 1), :]
        for row in range(12, 16):
            totals[(1,) + divmod(row, XY) + (SHARE,)] = jnp.zeros((16, 128), BF16)


    by_rows(x_in, x_rows)
    pl.semaphore_wait(barrier, len(peers))
    halos[0].start()
    for x in range(CX):
        windows[0, MAIN + x] = x_rows[x].astype(F32)
    shifts[...] = shift_matrix()
    bias_rows = jnp.concatenate([bias_in[...], jnp.zeros((128 - LAYERS, HID), F32)], axis=0)
    bias_col[...] = bias_rows.T
    for layer in range(LAYERS):
        columns(layer)
    spread_taps(cols, spread)
    for copy in loaded:
        copy.wait()
    prepare(0)
    forward(0)
    output(0)
    halos[1].start()
    prepare(1)
    for layer in range(LAYERS):
        prepare_back(layer)
    by_rows(cot_in, cot_rows)
    for x in range(CX):
        flow[x] = cot_rows[x].astype(F32) * (1.0 / 256.0)
    forward(1)
    backward(1)
    backward_norm(1)
    halos[2].start()
    sums[1].start(grad_w.at[1])
    kernel_grad(windows.at[1], conv_grad, grad_k, 64, True)
    passed = stretch_ahead()
    sums[1].to_plane()
    for x in range(CX):
        windows[1, MAIN + x] = conv_grad[x]
    halos[2].near(shifts, halo, windows.at[1])
    depthwise(windows.at[1], spread.at[1], conv, True, True)
    outer(2, 1, True)
    for x in range(CX):
        flow[x] = flow[x] + conv[x]
    sums[1].to_line()
    backward(0)
    sums[0].start(grad_w.at[0])
    backward_norm(0)
    sums[0].to_plane()
    sums[1].back_line()
    kernel_grad(windows.at[0], conv_grad, grad_k, 0, False)
    sums[0].start_extra(grad_k)
    sums[0].extra_to_plane()
    sums[0].to_line()
    sums[1].back_plane()
    sums[0].back_line()
    sums[0].back_plane()
    picked = stretch_share()
    sums[1].back_twin()
    sums[0].forward_twin()
    joined_copy = stretch_gather(picked)
    sums[0].end_twin()
    passed.wait()
    joined_copy.wait()
    stretch_result()
    for copy in picked:
        copy.wait_send()
    for each in halos + sums:
        each.close()


def whole_step(*operands):
    dma = pltpu.SemaphoreType.DMA
    vmem = pltpu.VMEM
    sums = ([dma((9,))] * 2 + [dma((7,))] * 8 + [dma((8,))] * 2 + [dma((7,))] * 2) * LAYERS
    return pl.pallas_call(
        step_kernel,
        out_shape=jax.ShapeDtypeStruct((LAYERS, 2, XY, SHARE + 1, 16, 128), BF16),
        in_specs=[pl.BlockSpec(memory_space=pltpu.SMEM)]
        + [pl.BlockSpec(memory_space=pltpu.VMEM)] * 9
        + [pl.BlockSpec(memory_space=pl.ANY)] * 4,
        out_specs=pl.BlockSpec(memory_space=pltpu.VMEM),
        scratch_shapes=[
            vmem((C * CX, CY), F32),
            vmem((CX, C, CY), BF16),
            vmem((CX, C, CY), BF16),
            vmem((2, LAYERS, C, HID), F32),
            vmem((2, LAYERS, C, HID), F32),
            vmem((C, 128), F32),
            vmem((128, 256), F32),
            vmem((LAYERS, C, 128), F32),
            vmem((HID, 128), F32),
            vmem((LAYERS, C, HID), BF16),
            vmem((LAYERS, HID, C), BF16),
            vmem((LAYERS, C, HID), BF16),
            vmem((LAYERS, HID, C), BF16),
            vmem((2 * CY, 6 * CY), BF16),
            vmem((LAYERS, 50, C, CY), F32),
            vmem((LAYERS, 7 * ROWS, C, CY), F32),
            vmem((ROWS, C, CY), BF16),
            vmem((CX, C, CY), F32),
            vmem((LAYERS, CX, C, CY), F32),
            vmem((LAYERS, CX, CY), F32),
            vmem((LAYERS, C, CELLS), BF16),
            vmem((HID, CELLS), F32),
            vmem((LAYERS, HID, CELLS), F32),
            vmem((LAYERS, HID, CELLS), BF16),
            vmem((CX, C, CY), F32),
            vmem((C, CELLS), BF16),
            vmem((HID, CELLS), BF16),
            vmem((CX, C, CY), F32),
            vmem((LAYERS, 2, C, HID), F32),
            vmem((C, 128), F32),
            vmem((2, CX, C, CY), BF16),
            vmem((3, FOLDED, CY), BF16),
            vmem((3, 2, 3, C, CY), BF16),
            vmem((3, 2, 3, FOLDED, CY), BF16),
            vmem((LAYERS, 80, 16, 128), BF16),
            vmem((LAYERS, 80, 16, 128), BF16),
            vmem((LAYERS, 80, 16, 128), F32),
            vmem((LAYERS, EW * ZT, 16, 128), F32),
            vmem((LAYERS, XY - 1, SHARE + 1, 16, 128), BF16),
            vmem((LAYERS, XY - 1, SHARE + 1, 16, 128), BF16),
            vmem((LAYERS, EW * ZT, 16, 128), BF16),
            vmem((LAYERS, EW - 1, ZT, 16, 128), BF16),
            vmem((LAYERS, EW * ZT, 16, 128), BF16),
            vmem((2, 16, 128), BF16),
            vmem((XY, 2, 16, 128), BF16),
            vmem((2, XY, 2, 16, 128), BF16),
            vmem((C, 128), F32),
            dma((3, 2 * CUTS + 6)),
            dma((3, 2 * CUTS + 6)),
            dma((2,)),
            dma((2,)),
            dma((2,)),
            dma((2,)),
            dma((8,)),
            dma((8,)),
        ]
        + sums,
        compiler_params=pltpu.CompilerParams(
            collective_id=0, has_side_effects=True, vmem_limit_bytes=60 * 2**20
        ),
    )(*operands)


def update_kernel(
    totals, win, wout_t, taps_in, new_in, new_out, new_k, cycle_in, cycle_out
):
    for layer in range(LAYERS):
        for tile in range(72):
            row, col = divmod(tile, 6)
            at = (layer, slice(16 * row, 16 * (row + 1)), slice(128 * col, 128 * (col + 1)))
            spot = divmod(tile, SHARE)
            new_in[at] = win[at] - STEP_RATE * totals[(layer, 0) + spot].astype(F32)
            new_out[at] = wout_t[at] - STEP_RATE * totals[(layer, 1) + spot].astype(F32)
    grads = [totals[0, half, tile, SHARE].astype(F32) for half in range(2) for tile in range(6)]
    taps = jnp.concatenate(grads, axis=0).T
    for layer in range(LAYERS):
        new_k[:, layer, :] = taps_in[:, layer, :] - STEP_RATE * taps[64 * layer : 64 * layer + 49]
    rows = [totals[(1,) + divmod(row, XY) + (SHARE,)].astype(F32) for row in range(12)]
    turned = jnp.concatenate(rows, axis=0).T
    cycle_in[...] = turned[0:64]
    cycle_out[...] = turned[64:128]


def update(totals, win, wout_t, taps):
    weights = jax.ShapeDtypeStruct((LAYERS, C, HID), F32)
    part = jax.ShapeDtypeStruct((64, C), F32)
    return pl.pallas_call(
        update_kernel,
        out_shape=[weights, weights, jax.ShapeDtypeStruct((49, LAYERS, C), F32), part, part],
        in_specs=[pl.BlockSpec(memory_space=pltpu.VMEM)] * 4,
        out_specs=[pl.BlockSpec(memory_space=pltpu.VMEM)] * 5,
        compiler_params=pltpu.CompilerParams(vmem_limit_bytes=40 * 2**20),
    )(totals, win, wout_t, taps)


def body(
    fields,
    cotangent,
    land_mask,
    stretch_index,
    depth_kernel,
    norm_gain,
    norm_bias,
    weight_in,
    bias_in,
    weight_out,
    bias_out,
    layer_scale,
    anchor_in,
    anchor_out,
):
    win = weight_in[0]
    wout_t = weight_out[0].transpose(0, 2, 1)
    taps = depth_kernel[0].transpose(2, 0, 1)
    totals = whole_step(
        stretch_index,
        fields.reshape(C * CX, CY),
        cotangent.reshape(C * CX, CY),
        land_mask,
        taps,
        norm_gain[0],
        norm_bias[0],
        bias_out[0],
        layer_scale[0],
        bias_in[0],
        win,
        wout_t,
        anchor_in,
        anchor_out.transpose(0, 2, 1),
    )
    new_in, new_out, new_k, cycle_in, cycle_out = update(totals, win, wout_t, taps)
    return (
        new_k.transpose(1, 2, 0)[None],
        new_in[None],
        new_out.transpose(0, 2, 1)[None],
        cycle_in.T[None],
        cycle_out[None],
    )


def solution(mesh):
    in_specs = (
        P("rep", None, "ew", "ns"),
        P("rep", None, "ew", "ns"),
        P("ew", "ns"),
        P(),
        P("rep", None, None, None),
        P("rep", None, None),
        P("rep", None, None),
        P("rep", None, None, None),
        P("rep", None, None),
        P("rep", None, None, None),
        P("rep", None, None),
        P("rep", None, None),
        P(),
        P(),
    )
    out_specs = (
        P("rep", None, None, None),
        P("rep", None, None, None),
        P("rep", None, None, None),
        P("rep", None, None),
        P("rep", None, None),
    )
    return jax.shard_map(body, mesh=mesh, in_specs=in_specs, out_specs=out_specs, check_vma=False)
```

```python
import jax
import jax.numpy as jnp
from jax import lax
from jax.experimental import pallas as pl
from jax.experimental.pallas import tpu as pltpu
from jax.sharding import PartitionSpec as P

EPSILON = 1e-06
STEP_RATE = 0.1
GELU_C = 0.7978845608028654
GELU_D = 0.044715

MESH = pl.DeviceIdType.MESH
F32 = jnp.float32
BF16 = jnp.bfloat16
C = 192
HID = 768
LAYERS = 2
CX = 4
CY = 128
CELLS = CX * CY
ROWS = CX + 6
BLOCKS = C // 8
FOLD = 4
CUTS = 6
CUT = C // CUTS
FOLDED = C // FOLD
XY = 8
EW = 8
SHIFTED = (0, 1, 2, 4, 5, 6)
PLANE_ORDER = [2, 6, 1, 3, 5, 7, 4]
LINE_ORDER = [4, 3, 5, 2, 6, 1, 7]
NS = 16
ZT = 2
GAIN, SHIFT, OUT_BIAS, SCALE = 49, 50, 51, 52
SHARE = 9
MAIN = 3 * ROWS + 3
SHARES = (10, 9)


def remote(src, dst, send_sem, recv_sem, device):
    return pltpu.make_async_remote_copy(
        src_ref=src,
        dst_ref=dst,
        send_sem=send_sem,
        recv_sem=recv_sem,
        device_id=device,
        device_id_type=MESH,
    )


def lanes_of(shape):
    return lax.broadcasted_iota(jnp.int32, shape, 1)


def dot(left, right):
    return jnp.dot(left, right, preferred_element_type=F32)


def dot_cells(left, right):
    return lax.dot_general(left, right, (((1,), (1,)), ((), ())), preferred_element_type=F32)


class Place:
    def __init__(self):
        self.rep = lax.axis_index("rep")
        self.z = lax.axis_index("ew")
        self.ns = lax.axis_index("ns")
        self.core = lax.rem(self.ns, 2)
        self.chip = self.ns // 2

    def twin(self):
        return (self.rep, self.z, 2 * self.chip + 1 - self.core)

    def in_plane(self, step):
        return (self.rep, self.z, 2 * lax.rem(self.chip + step, XY) + self.core)

    def on_line(self, step):
        return (self.rep, lax.rem(self.z + step, EW), self.ns)

    def beside(self, step_z, step_ns):
        return (
            self.rep,
            lax.rem(self.z + EW + step_z, EW),
            lax.rem(self.ns + NS + step_ns, NS),
        )


AROUND = [(dz, dn) for dn in (1, -1) for dz in (-1, 0, 1)]


class Halo:
    def __init__(self, place, turn, rows, out_edges, in_rows, in_edges, sent, came):
        self.place = place
        self.rows = rows
        self.out_edges = out_edges.at[turn]
        self.in_rows = in_rows.at[turn]
        self.in_edges = in_edges.at[turn]
        self.sent = sent.at[turn]
        self.came = came.at[turn]
        self.row_copies = []
        self.edge_copies = []

    def send_rows(self, cut):
        at = pl.ds(CUT * cut, CUT)
        for number, (first, step) in enumerate(((1, 1), (0, -1))):
            copy = remote(
                self.rows.at[pl.ds(first, 3), at],
                self.in_rows.at[number, :, at],
                self.sent.at[2 * cut + number],
                self.came.at[2 * cut + number],
                self.place.beside(step, 0),
            )
            copy.start()
            self.row_copies.append(copy)

    def start(self):
        place = self.place
        slot = ((lanes_of((FOLDED, CY)) + 4) % CY) // 8
        folded = jnp.zeros((FOLDED, CY), F32)
        for x in range(CX):
            row = self.rows[x].astype(F32)
            for part in range(FOLD):
                piece = row[FOLDED * part : FOLDED * (part + 1), :]
                number = 4 * part + x
                moved = pltpu.roll(piece, 8 * number, 1) if number else piece
                folded = jnp.where(slot == number, moved, folded)
        self.out_edges[...] = folded.astype(BF16)
        for number, (dz, dn) in enumerate(AROUND):
            side = 0 if dn == 1 else 1
            copy = remote(
                self.out_edges,
                self.in_edges.at[side, 1 - dz],
                self.sent.at[2 * CUTS + number],
                self.came.at[2 * CUTS + number],
                place.beside(dz, dn),
            )
            copy.start()
            self.edge_copies.append(copy)
        for cut in range(CUTS):
            self.send_rows(cut)

    def near(self, shifts, halo, windows):
        self.rims(halo, (1,))
        cells = jnp.concatenate(
            [self.rows[...].reshape(CX * C, CY), halo[3 : 3 + CX].reshape(CX * C, CY)], axis=1
        )
        moved = dot(cells, shifts[...])
        for place, col in enumerate(SHIFTED):
            start = col * ROWS + 3
            part = moved[:, CY * place : CY * (place + 1)]
            windows[start : start + CX] = part.reshape(CX, C, CY)

    def rims(self, halo, indices):
        for copy, (dz, _) in zip(self.edge_copies, AROUND):
            if 1 - dz in indices:
                copy.wait_recv()
        keep_left = (self.place.ns > 0).astype(F32)
        keep_right = (self.place.ns < NS - 1).astype(F32)
        low = (lanes_of((FOLDED, CY)) + 4) % 8 < 4
        for index in indices:
            edges = jnp.where(
                low,
                self.in_edges[0, index].astype(F32) * keep_left,
                self.in_edges[1, index].astype(F32) * keep_right,
            )
            for x in range(CX):
                row = (x - 1, x + 3, x + 7)[index]
                if (index == 0 and x == 0) or (index == 2 and x == 3):
                    continue
                for part in range(FOLD):
                    number = 4 * part + x
                    moved = pltpu.roll(edges, CY - 8 * number, 1) if number else edges
                    halo[row, FOLDED * part : FOLDED * (part + 1), :] = moved.astype(BF16)

    def far(self, shifts, halo, windows, cut):
        for copy in self.row_copies[2 * cut : 2 * cut + 2]:
            copy.wait_recv()
        at = slice(CUT * cut, CUT * (cut + 1))
        cells = []
        for side, first in ((0, 0), (1, CX + 3)):
            rows = self.in_rows[side, :, at]
            rims = halo[first : first + 3, at]
            cells.append(
                jnp.concatenate([rows.reshape(3 * CUT, CY), rims.reshape(3 * CUT, CY)], axis=1)
            )
            start = 3 * ROWS + first
            windows[start : start + 3, at] = rows.astype(F32)
        moved = dot(jnp.concatenate(cells, axis=0), shifts[...])
        for side, first in ((0, 0), (1, CX + 3)):
            for place, col in enumerate(SHIFTED):
                start = col * ROWS + first
                part = moved[3 * CUT * side : 3 * CUT * (side + 1), CY * place : CY * (place + 1)]
                windows[start : start + 3, at] = part.reshape(3, CUT, CY)

    def close(self):
        for copy in self.row_copies + self.edge_copies:
            copy.wait_send()


def shift_matrix():
    source = lax.broadcasted_iota(jnp.int32, (2 * CY, CY), 0)
    lane = lanes_of((2 * CY, CY))
    parts = []
    for col in SHIFTED:
        wanted = lane + (col - 3)
        hit = (source == wanted) | (source == wanted + 2 * CY)
        parts.append(hit.astype(F32).astype(BF16))
    return jnp.concatenate(parts, axis=1)


def spread_taps(cols, out):
    parts = []
    for layer in range(LAYERS):
        taps = cols[layer]
        high = taps.astype(BF16).astype(F32)
        middle = (taps - high).astype(BF16).astype(F32)
        parts.append(
            jnp.concatenate([high + pltpu.roll(middle, 64, 1), taps - high - middle], axis=1)
        )
    left = jnp.concatenate(parts, axis=0).astype(BF16)
    source = lax.broadcasted_iota(jnp.int32, (256, 128), 0) % 64
    for tap in range(0, 50, 2):
        picks = [(source == tap + side).astype(F32).astype(BF16) for side in range(2)]
        moved = dot(left, jnp.concatenate(picks, axis=1))
        for layer in range(LAYERS):
            rows = slice(C * layer, C * (layer + 1))
            out[layer, tap] = moved[rows, 0:CY]
            out[layer, tap + 1] = moved[rows, CY : 2 * CY]


def depthwise(windows, spread, out, reverse, own, first=0, blocks=BLOCKS):
    @pl.loop(first, first + blocks, unroll=4)
    def _(block):
        at = pl.ds(block * 8, 8)
        total = [None if own else out[x, at, :] for x in range(CX)]
        used = [row for row in range(ROWS) if (3 <= row < 3 + CX) == own]
        for col in range(7):
            rows = {row: windows[col * ROWS + row, at, :] for row in used}
            part = [None] * CX
            for tap_row in range(7):
                if not any(x + tap_row in rows for x in range(CX)):
                    continue
                tap = 7 * tap_row + col
                weight = spread[48 - tap if reverse else tap, at, :]
                for x in range(CX):
                    if x + tap_row in rows:
                        term = weight * rows[x + tap_row]
                        part[x] = term if part[x] is None else part[x] + term
            for x in range(CX):
                if part[x] is not None:
                    total[x] = part[x] if total[x] is None else total[x] + part[x]
        for x in range(CX):
            out[x, at, :] = total[x]


def kernel_grad(windows, conv_grad, out, lane_base, first):
    @pl.loop(0, BLOCKS, unroll=8)
    def _(block):
        at = pl.ds(block * 8, 8)
        lane = lanes_of((8, CY))
        grads = [conv_grad[x, at, :] for x in range(CX)]
        result = jnp.zeros((8, CY), F32)
        for col in range(7):
            rows = [windows[col * ROWS + row, at, :] for row in range(ROWS)]
            for tap_row in range(7):
                total = grads[0] * rows[tap_row]
                for x in range(1, CX):
                    total = total + grads[x] * rows[x + tap_row]
                tap = 7 * tap_row + col
                result = jnp.where(
                    lane == tap + lane_base, jnp.sum(total, axis=1, keepdims=True), result
                )
        if first:
            out[at, :] = result
        else:
            out[at, :] = out[at, :] + result


class Sum:
    def __init__(
        self, place, tiles, send1, recv1, own, mine, send2, recv2, send3, recv3, line, total, sems
    ):
        self.place = place
        self.tiles = tiles
        self.send1, self.recv1, self.own, self.mine = send1, recv1, own, mine
        self.send2, self.recv2, self.send3, self.recv3 = send2, recv2, send3, recv3
        self.line = line
        self.total = total
        self.sems = sems
        self.started = []
        self.extra = None

    def go(self, copy):
        copy.start()
        self.started.append(copy)
        return copy

    def pair(self, phase, step):
        return self.sems[2 * phase].at[step], self.sems[2 * phase + 1].at[step]

    def pack(self, grads, half, dst):
        @pl.loop(0, 12, unroll=2)
        def _(row):
            for col in range(6):
                dst[row * 6 + col] = grads[
                    half, pl.ds(row * 16, 16), 128 * col : 128 * (col + 1)
                ].astype(dst.dtype)

    def pack_extra(self, extra, half, dst):
        for block in range(6):
            dst[72 + block] = extra[pl.ds(half * 96 + 16 * block, 16), :].astype(dst.dtype)
        dst[78:80] = jnp.zeros((2, 16, 128), dst.dtype)

    def chunk(self, step):
        return lax.rem(self.place.chip + step, XY)

    def share(self, step):
        return pl.ds(SHARE * self.chunk(step), SHARE)

    def start(self, grads):
        core = self.place.core
        self.pack(grads, 1 - core, self.send1)
        self.first = []
        for step in PLANE_ORDER + [0]:
            part = self.share(step)
            copy = remote(
                self.send1.at[part], self.recv1.at[part], *self.pair(0, step), self.place.twin()
            )
            self.first.append((step, self.go(copy)))
        self.pack(grads, core, self.own)

    def start_extra(self, extra):
        core = self.place.core
        self.pack_extra(extra, 1 - core, self.send1)
        part = pl.ds(72, 8)
        self.extra = self.go(
            remote(self.send1.at[part], self.recv1.at[part], *self.pair(0, 8), self.place.twin())
        )
        self.pack_extra(extra, core, self.own)

    def to_plane(self):
        self.second = []
        self.mine[...] = jnp.zeros_like(self.mine)
        for step, copy in self.first:
            copy.wait_recv()
            part = self.own[self.share(step)] + self.recv1[self.share(step)].astype(F32)
            if step == 0:
                self.mine[0:SHARE] = part
            else:
                self.send2[step - 1, 0:SHARE] = part.astype(BF16)
                copy = remote(
                    self.send2.at[step - 1, pl.ds(0, SHARE)],
                    self.recv2.at[step - 1, pl.ds(0, SHARE)],
                    *self.pair(1, step - 1),
                    self.place.in_plane(step),
                )
                self.second.append(self.go(copy))

    def extra_to_plane(self):
        self.extra.wait_recv()
        for step in PLANE_ORDER + [0]:
            spot = 72 + self.chunk(step)
            part = self.own[spot] + self.recv1[spot].astype(F32)
            if step == 0:
                self.mine[SHARE] = part
            else:
                self.send2[step - 1, SHARE] = part.astype(BF16)
                copy = remote(
                    self.send2.at[step - 1, pl.ds(SHARE, 1)],
                    self.recv2.at[step - 1, pl.ds(SHARE, 1)],
                    *self.pair(6, step - 1),
                    self.place.in_plane(step),
                )
                self.second.append(self.go(copy))

    def stretch(self, step):
        return pl.ds(ZT * lax.rem(self.place.z + step, EW), ZT)

    def to_line(self):
        for copy in self.second:
            copy.wait_recv()
        part = self.mine[0 : self.tiles]
        for step in range(XY - 1):
            part = part + self.recv2[step, 0 : self.tiles].astype(F32)
        self.mine[0 : self.tiles] = part
        self.send3[...] = self.mine[...].astype(BF16)
        self.third = []
        for step in range(1, EW):
            copy = remote(
                self.send3.at[self.stretch(step)],
                self.recv3.at[step - 1],
                *self.pair(2, step - 1),
                self.place.on_line(step),
            )
            self.third.append(copy)
        for step in LINE_ORDER:
            self.go(self.third[step - 1])

    def back_line(self):
        for copy in self.third:
            copy.wait_recv()
        part = self.mine[self.stretch(0)]
        for step in range(EW - 1):
            part = part + self.recv3[step].astype(F32)
        here = self.line.at[self.stretch(0)]
        here[...] = part.astype(BF16)
        self.fourth = []
        for step in range(1, EW):
            copy = remote(here, here, *self.pair(3, step - 1), self.place.on_line(step))
            self.fourth.append(copy)
        for step in LINE_ORDER:
            self.go(self.fourth[step - 1])

    def back_plane(self):
        for copy in self.fourth:
            copy.wait_recv()
        core, chip = self.place.core, self.place.chip
        used = pl.ds(0, self.tiles)
        share, mine = self.line.at[used], self.total.at[core, chip, used]
        self.fifth = []
        for step in range(1, XY):
            copy = remote(share, mine, *self.pair(4, step - 1), self.place.in_plane(step))
            self.fifth.append(self.go(copy))
        self.sixth = [self.go(remote(share, mine, *self.pair(5, 0), self.place.twin()))]
        mine[...] = share[...]

    def back_twin(self):
        self.forward_twin()
        self.end_twin()

    def forward_twin(self):
        for step, copy in enumerate(self.fifth):
            copy.wait_recv()
            came = self.total.at[
                self.place.core,
                lax.rem(self.place.chip + XY - (step + 1), XY),
                pl.ds(0, self.tiles),
            ]
            copy = remote(came, came, *self.pair(5, step + 1), self.place.twin())
            self.sixth.append(self.go(copy))

    def end_twin(self):
        for copy in self.sixth:
            copy.wait_recv()

    def close(self):
        for copy in self.started:
            copy.wait_send()


def step_kernel(
    index,
    x_in,
    cot_in,
    mask_in,
    taps_in,
    gain_in,
    shift_in,
    out_bias_in,
    scale_in,
    bias_in,
    win_hbm,
    wout_hbm,
    anchor_in,
    anchor_out,
    totals,
    cells_t,
    x_rows,
    cot_rows,
    weights,
    anchors,
    ahead,
    rows_t,
    cols,
    bias_col,
    win_b,
    win_tb,
    wout_tb,
    wout_b,
    shifts,
    spread,
    windows,
    halo,
    conv,
    normed,
    inv_std,
    norm_b,
    hidden,
    slope,
    act_b,
    flow,
    back_b,
    hid_b,
    conv_grad,
    grad_w,
    grad_k,
    out_rows,
    out_edges,
    in_rows,
    in_edges,
    send1,
    recv1,
    own,
    mine,
    send2,
    recv2,
    send3,
    recv3,
    line,
    picks,
    came,
    tiles_by,
    ahead_came,
    halo_sent,
    halo_came,
    weight_sem,
    anchor_sem,
    ahead_sem,
    tiles_sem,
    pick_sent,
    pick_came,
    *sems,
):
    place = Place()
    barrier = pltpu.get_barrier_semaphore()
    partner = (1 - place.rep, place.z, place.ns)
    peers = [place.twin()]
    peers += [(1 - place.rep,) + place.in_plane(d)[1:] for d in range(XY)]
    peers += [place.in_plane(d) for d in range(1, XY)]
    peers += [place.on_line(d) for d in range(1, EW)]
    peers += [place.beside(dz, dn) for dz, dn in AROUND]
    for peer in peers:
        pl.semaphore_signal(barrier, inc=1, device_id=peer, device_id_type=MESH)
    fetched = [
        pltpu.make_async_copy(anchor_in, anchors.at[0], anchor_sem.at[0]),
        pltpu.make_async_copy(anchor_out, anchors.at[1], anchor_sem.at[1]),
    ]
    loaded = [
        pltpu.make_async_copy(win_hbm, weights.at[0], weight_sem.at[0]),
        pltpu.make_async_copy(wout_hbm, weights.at[1], weight_sem.at[1]),
    ]
    for copy in loaded + fetched:
        copy.start()
    win, wout_t = weights.at[0], weights.at[1]

    def lanes(x):
        return slice(CY * x, CY * (x + 1))

    halos = [
        Halo(
            place,
            turn,
            (x_rows, out_rows.at[0], out_rows.at[1])[turn],
            out_edges,
            in_rows,
            in_edges,
            halo_sent,
            halo_came,
        )
        for turn in range(3)
    ]
    sums = [
        Sum(
            place,
            SHARES[layer],
            send1.at[layer],
            recv1.at[layer],
            own.at[layer],
            mine.at[layer],
            send2.at[layer],
            recv2.at[layer],
            send3.at[layer],
            recv3.at[layer],
            line.at[layer],
            totals.at[layer],
            sems[14 * layer : 14 * (layer + 1)],
        )
        for layer in range(LAYERS)
    ]

    def columns(layer):
        rows_t[...] = jnp.zeros_like(rows_t)
        rows_t[0:49, 0:C] = taps_in[:, layer, :]
        for row, vector in (
            (GAIN, gain_in),
            (SHIFT, shift_in),
            (OUT_BIAS, out_bias_in),
            (SCALE, scale_in),
        ):
            rows_t[row : row + 1, 0:C] = vector[layer : layer + 1, :]
        cols[layer] = rows_t[...].T[:C]

    def prepare(layer):
        win_tb[layer] = win[layer].T.astype(BF16)
        wout_tb[layer] = wout_t[layer].astype(BF16)

    def prepare_back(layer):
        win_b[layer] = win[layer].astype(BF16)
        wout_b[layer] = wout_t[layer].T.astype(BF16)

    ocean = [mask_in[x : x + 1, :].astype(F32) for x in range(CX)]

    def column(layer, which):
        return cols[layer, :, which : which + 1]

    def outer(turn, layer, reverse):
        halos[turn].rims(halo, (0, 2))
        for cut in range(CUTS):
            halos[turn].far(shifts, halo, windows.at[layer], cut)
            part = (cut * (CUT // 8), CUT // 8)
            depthwise(windows.at[layer], spread.at[layer], conv, reverse, False, *part)

    def forward(layer):
        halos[layer].near(shifts, halo, windows.at[layer])
        depthwise(windows.at[layer], spread.at[layer], conv, False, True)
        outer(layer, layer, False)
        for x in range(CX):
            cells = conv[x]
            centered = cells - jnp.mean(cells, axis=0, keepdims=True)
            inv = lax.rsqrt(jnp.mean(centered * centered, axis=0, keepdims=True) + EPSILON)
            unit = centered * inv
            inv_std[layer, x : x + 1, :] = inv
            normed[layer, x] = unit
            norm_b[layer, :, lanes(x)] = (
                unit * column(layer, GAIN) + column(layer, SHIFT)
            ).astype(BF16)
        hidden[...] = dot(win_tb[layer], norm_b[layer])

        @pl.loop(0, HID // 192, unroll=4)
        def _(block):
            at = pl.ds(block * 192, 192)
            pre = hidden[at, :] + bias_col[at, layer : layer + 1]
            bend = (GELU_C * GELU_D) * (pre * pre)
            gate = 0.5 + 0.5 * jnp.tanh(pre * (GELU_C + bend))
            value = pre * gate
            act_b[layer, at, :] = value.astype(BF16)
            slope[layer, at, :] = gate + 2.0 * value * (1.0 - gate) * (GELU_C + 3.0 * bend)

    def output(layer):
        branch = dot(wout_tb[layer], act_b[layer])
        for x in range(CX):
            inner = branch[:, lanes(x)] + column(layer, OUT_BIAS)
            value = ocean[x] * (windows[layer, MAIN + x] + column(layer, SCALE) * inner)
            value = value.astype(BF16)
            out_rows[0, x] = value
            windows[layer + 1, MAIN + x] = value.astype(F32)

    def backward(layer):
        for x in range(CX):
            masked = ocean[x] * flow[x]
            flow[x] = masked
            back_b[:, lanes(x)] = (masked * column(layer, SCALE)).astype(BF16)
        grad_w[layer, 1] = dot_cells(back_b[...], act_b[layer])
        hidden[...] = dot(wout_b[layer], back_b[...])

        @pl.loop(0, HID // 192, unroll=4)
        def _(block):
            at = pl.ds(block * 192, 192)
            hid_b[at, :] = (hidden[at, :] * slope[layer, at, :]).astype(BF16)

        grad_w[layer, 0] = dot_cells(norm_b[layer], hid_b[...])

    def backward_norm(layer):
        norm_grad = dot(win_b[layer], hid_b[...])
        for x in range(CX):
            part = norm_grad[:, lanes(x)] * column(layer, GAIN)
            unit = normed[layer, x]
            mean_grad = jnp.mean(part, axis=0, keepdims=True)
            mean_cross = jnp.mean(part * unit, axis=0, keepdims=True)
            value = inv_std[layer, x : x + 1, :] * (part - mean_grad - unit * mean_cross)
            conv_grad[x] = value
            if layer > 0:
                out_rows[1, x] = value.astype(BF16)

    def by_rows(cells_in, out):
        cells_t[...] = cells_in[...].astype(F32)
        for x in range(CX):
            out[x] = cells_t[pl.ds(x, C, stride=CX), :].astype(BF16)

    def hits(shape):
        spot = jnp.full(shape, index[0] // 2, jnp.int32)
        return [
            (layer, col, spot == 6 * layer + col) for layer in range(LAYERS) for col in range(6)
        ]

    def joined(first, second):
        odd = jnp.full((C, 128), lax.rem(index[0], 2), jnp.int32) == 1
        first = jnp.where(odd, pltpu.roll(first, 64, 1), first)
        second = jnp.where(odd, second, pltpu.roll(second, 64, 1))
        return jnp.where(lanes_of((C, 128)) < 64, first, second)

    def stretch_ahead():
        for copy in fetched:
            copy.wait()
        chosen = [jnp.zeros((C, 128), F32), jnp.zeros((C, 128), F32)]
        for layer, col, hit in hits((C, 128)):
            at = (layer, slice(0, C), slice(128 * col, 128 * (col + 1)))
            for mat, weights in enumerate((win, wout_t)):
                chosen[mat] = jnp.where(hit, anchors[(mat,) + at] - weights[at], chosen[mat])
        ahead[...] = joined(*chosen)
        copy = remote(ahead, ahead_came, ahead_sem.at[0], ahead_sem.at[1], partner)
        copy.start()
        return copy

    def stretch_share():
        for slot in range(2):
            picked = jnp.zeros((16, 128), BF16)
            for layer, col, hit in hits((16, 128)):
                at = lax.rem(col + 3 * place.chip, 6) + 6 * slot
                picked = jnp.where(hit, line[layer, at], picked)
            picks[slot] = picked
        copies = []
        for step in range(XY):
            z, ns = place.in_plane(step)[1:]
            copies.append(
                remote(
                    picks, came.at[step], pick_sent.at[step], pick_came.at[step], (1 - place.rep, z, ns)
                )
            )
        for copy in copies:
            copy.start()
        return copies

    def stretch_gather(copies):
        for step, copy in enumerate(copies):
            copy.wait_recv()
            source = lax.rem(place.chip + XY - step, XY)
            tiles_by[place.core, source] = came[step]
        part = tiles_by.at[place.core]
        copy = remote(part, part, tiles_sem.at[0], tiles_sem.at[1], place.twin())
        copy.start()
        return copy

    def stretch_result():
        chosen = [jnp.zeros((C, 128), BF16), jnp.zeros((C, 128), BF16)]
        spot = lax.rem(jnp.full((C, 128), index[0] // 2, jnp.int32), 6)
        for col in range(6):
            for mat in range(2):
                rows = []
                for row in range(12):
                    chip, inside = divmod(6 * row + col, SHARE)
                    rows.append(tiles_by[mat, chip, inside // 6])
                rows = jnp.concatenate(rows, axis=0)
                chosen[mat] = jnp.where(spot == col, rows, chosen[mat])
        grads = joined(chosen[0].astype(F32), chosen[1].astype(F32))
        result = (ahead_came[...] + STEP_RATE * grads).astype(BF16)
        for row in range(12):
            spot = (1,) + divmod(row, XY) + (SHARE,)
            totals[spot] = result[16 * row : 16 * (row + 1), :]
        for row in range(12, 16):
            totals[(1,) + divmod(row, XY) + (SHARE,)] = jnp.zeros((16, 128), BF16)


    by_rows(x_in, x_rows)
    pl.semaphore_wait(barrier, len(peers))
    halos[0].start()
    for x in range(CX):
        windows[0, MAIN + x] = x_rows[x].astype(F32)
    shifts[...] = shift_matrix()
    bias_rows = jnp.concatenate([bias_in[...], jnp.zeros((128 - LAYERS, HID), F32)], axis=0)
    bias_col[...] = bias_rows.T
    for layer in range(LAYERS):
        columns(layer)
    spread_taps(cols, spread)
    for copy in loaded:
        copy.wait()
    prepare(0)
    forward(0)
    output(0)
    halos[1].start()
    prepare(1)
    for layer in range(LAYERS):
        prepare_back(layer)
    by_rows(cot_in, cot_rows)
    for x in range(CX):
        flow[x] = cot_rows[x].astype(F32) * (1.0 / 256.0)
    forward(1)
    backward(1)
    backward_norm(1)
    halos[2].start()
    sums[1].start(grad_w.at[1])
    kernel_grad(windows.at[1], conv_grad, grad_k, 64, True)
    passed = stretch_ahead()
    sums[1].to_plane()
    for x in range(CX):
        windows[1, MAIN + x] = conv_grad[x]
    halos[2].near(shifts, halo, windows.at[1])
    depthwise(windows.at[1], spread.at[1], conv, True, True)
    outer(2, 1, True)
    for x in range(CX):
        flow[x] = flow[x] + conv[x]
    sums[1].to_line()
    backward(0)
    sums[0].start(grad_w.at[0])
    backward_norm(0)
    sums[0].to_plane()
    sums[1].back_line()
    kernel_grad(windows.at[0], conv_grad, grad_k, 0, False)
    sums[0].start_extra(grad_k)
    sums[0].extra_to_plane()
    sums[0].to_line()
    sums[1].back_plane()
    sums[0].back_line()
    sums[0].back_plane()
    picked = stretch_share()
    sums[1].back_twin()
    sums[0].forward_twin()
    joined_copy = stretch_gather(picked)
    sums[0].end_twin()
    passed.wait()
    joined_copy.wait()
    stretch_result()
    for copy in picked:
        copy.wait_send()
    for each in halos + sums:
        each.close()


def whole_step(*operands):
    dma = pltpu.SemaphoreType.DMA
    vmem = pltpu.VMEM
    sums = ([dma((9,))] * 2 + [dma((7,))] * 8 + [dma((8,))] * 2 + [dma((7,))] * 2) * LAYERS
    return pl.pallas_call(
        step_kernel,
        out_shape=jax.ShapeDtypeStruct((LAYERS, 2, XY, SHARE + 1, 16, 128), BF16),
        in_specs=[pl.BlockSpec(memory_space=pltpu.SMEM)]
        + [pl.BlockSpec(memory_space=pltpu.VMEM)] * 9
        + [pl.BlockSpec(memory_space=pl.ANY)] * 4,
        out_specs=pl.BlockSpec(memory_space=pltpu.VMEM),
        scratch_shapes=[
            vmem((C * CX, CY), F32),
            vmem((CX, C, CY), BF16),
            vmem((CX, C, CY), BF16),
            vmem((2, LAYERS, C, HID), F32),
            vmem((2, LAYERS, C, HID), F32),
            vmem((C, 128), F32),
            vmem((128, 256), F32),
            vmem((LAYERS, C, 128), F32),
            vmem((HID, 128), F32),
            vmem((LAYERS, C, HID), BF16),
            vmem((LAYERS, HID, C), BF16),
            vmem((LAYERS, C, HID), BF16),
            vmem((LAYERS, HID, C), BF16),
            vmem((2 * CY, 6 * CY), BF16),
            vmem((LAYERS, 50, C, CY), F32),
            vmem((LAYERS, 7 * ROWS, C, CY), F32),
            vmem((ROWS, C, CY), BF16),
            vmem((CX, C, CY), F32),
            vmem((LAYERS, CX, C, CY), F32),
            vmem((LAYERS, CX, CY), F32),
            vmem((LAYERS, C, CELLS), BF16),
            vmem((HID, CELLS), F32),
            vmem((LAYERS, HID, CELLS), F32),
            vmem((LAYERS, HID, CELLS), BF16),
            vmem((CX, C, CY), F32),
            vmem((C, CELLS), BF16),
            vmem((HID, CELLS), BF16),
            vmem((CX, C, CY), F32),
            vmem((LAYERS, 2, C, HID), F32),
            vmem((C, 128), F32),
            vmem((2, CX, C, CY), BF16),
            vmem((3, FOLDED, CY), BF16),
            vmem((3, 2, 3, C, CY), BF16),
            vmem((3, 2, 3, FOLDED, CY), BF16),
            vmem((LAYERS, 80, 16, 128), BF16),
            vmem((LAYERS, 80, 16, 128), BF16),
            vmem((LAYERS, 80, 16, 128), F32),
            vmem((LAYERS, EW * ZT, 16, 128), F32),
            vmem((LAYERS, XY - 1, SHARE + 1, 16, 128), BF16),
            vmem((LAYERS, XY - 1, SHARE + 1, 16, 128), BF16),
            vmem((LAYERS, EW * ZT, 16, 128), BF16),
            vmem((LAYERS, EW - 1, ZT, 16, 128), BF16),
            vmem((LAYERS, EW * ZT, 16, 128), BF16),
            vmem((2, 16, 128), BF16),
            vmem((XY, 2, 16, 128), BF16),
            vmem((2, XY, 2, 16, 128), BF16),
            vmem((C, 128), F32),
            dma((3, 2 * CUTS + 6)),
            dma((3, 2 * CUTS + 6)),
            dma((2,)),
            dma((2,)),
            dma((2,)),
            dma((2,)),
            dma((8,)),
            dma((8,)),
        ]
        + sums,
        compiler_params=pltpu.CompilerParams(
            collective_id=0, has_side_effects=True, vmem_limit_bytes=60 * 2**20
        ),
    )(*operands)


def update_kernel(
    totals, win, wout_t, taps_in, new_in, new_out, new_k, cycle_in, cycle_out
):
    for layer in range(LAYERS):
        for tile in range(72):
            row, col = divmod(tile, 6)
            at = (layer, slice(16 * row, 16 * (row + 1)), slice(128 * col, 128 * (col + 1)))
            spot = divmod(tile, SHARE)
            new_in[at] = win[at] - STEP_RATE * totals[(layer, 0) + spot].astype(F32)
            new_out[at] = wout_t[at] - STEP_RATE * totals[(layer, 1) + spot].astype(F32)
    grads = [totals[0, half, tile, SHARE].astype(F32) for half in range(2) for tile in range(6)]
    taps = jnp.concatenate(grads, axis=0).T
    for layer in range(LAYERS):
        new_k[:, layer, :] = taps_in[:, layer, :] - STEP_RATE * taps[64 * layer : 64 * layer + 49]
    rows = [totals[(1,) + divmod(row, XY) + (SHARE,)].astype(F32) for row in range(12)]
    turned = jnp.concatenate(rows, axis=0).T
    cycle_in[...] = turned[0:64]
    cycle_out[...] = turned[64:128]


def update(totals, win, wout_t, taps):
    weights = jax.ShapeDtypeStruct((LAYERS, C, HID), F32)
    part = jax.ShapeDtypeStruct((64, C), F32)
    return pl.pallas_call(
        update_kernel,
        out_shape=[weights, weights, jax.ShapeDtypeStruct((49, LAYERS, C), F32), part, part],
        in_specs=[pl.BlockSpec(memory_space=pltpu.VMEM)] * 4,
        out_specs=[pl.BlockSpec(memory_space=pltpu.VMEM)] * 5,
        compiler_params=pltpu.CompilerParams(vmem_limit_bytes=40 * 2**20),
    )(totals, win, wout_t, taps)


def body(
    fields,
    cotangent,
    land_mask,
    stretch_index,
    depth_kernel,
    norm_gain,
    norm_bias,
    weight_in,
    bias_in,
    weight_out,
    bias_out,
    layer_scale,
    anchor_in,
    anchor_out,
):
    win = weight_in[0]
    wout_t = weight_out[0].transpose(0, 2, 1)
    taps = depth_kernel[0].transpose(2, 0, 1)
    totals = whole_step(
        stretch_index,
        fields.reshape(C * CX, CY),
        cotangent.reshape(C * CX, CY),
        land_mask,
        taps,
        norm_gain[0],
        norm_bias[0],
        bias_out[0],
        layer_scale[0],
        bias_in[0],
        win,
        wout_t,
        anchor_in,
        anchor_out.transpose(0, 2, 1),
    )
    new_in, new_out, new_k, cycle_in, cycle_out = update(totals, win, wout_t, taps)
    return (
        new_k.transpose(1, 2, 0)[None],
        new_in[None],
        new_out.transpose(0, 2, 1)[None],
        cycle_in.T[None],
        cycle_out[None],
    )


def solution(mesh):
    in_specs = (
        P("rep", None, "ew", "ns"),
        P("rep", None, "ew", "ns"),
        P("ew", "ns"),
        P(),
        P("rep", None, None, None),
        P("rep", None, None),
        P("rep", None, None),
        P("rep", None, None, None),
        P("rep", None, None),
        P("rep", None, None, None),
        P("rep", None, None),
        P("rep", None, None),
        P(),
        P(),
    )
    out_specs = (
        P("rep", None, None, None),
        P("rep", None, None, None),
        P("rep", None, None, None),
        P("rep", None, None),
        P("rep", None, None),
    )
    return jax.shard_map(body, mesh=mesh, in_specs=in_specs, out_specs=out_specs, check_vma=False)
```
